256 devices in a mesh: seq: 32 (over z, y), mp: 8 (over x, core).
Axes of the slice: x: 4, y: 4, z: 8, core: 2. Of those that a mesh axis runs over, the one named last changes fastest.
Arguments:
- x_in: float32 [16384, 8192], P('seq', 'mp'), may hold values from -6 to 6
- dy_out: float32 [16384, 8192], P('seq', 'mp'), may hold values from -3 to 3
- b_in: float32 [16384, 128], P('seq'), may hold values from -0.18 to 0.18
- c_in: float32 [16384, 128], P('seq'), may hold values from -0.18 to 0.18
- log_decay: float32 [128, 16384], P('mp', 'seq'), may hold values from -1 to 0
- parents: int32 [32], replicated, may hold values from -1 to 30, as said below
- lengths: int32 [32], replicated, may hold values from 128 to 512, as said below
Outputs:
- x_grad: float32 [16384, 8192], P('seq', 'mp')
- b_grad: float32 [16384, 128], P('seq')
- c_grad: float32 [16384, 128], P('seq')
- decay_grad: float32 [128, 16384], P('mp', 'seq')
The draws below stay inside these ranges and needn't reach their ends.
Inputs may be any that keep to these rules, and one draw needn't show every extreme that they name: parents[b] is an earlier block for every block b after the first; block 0 has none; the last block resumes from the block just before it. `lengths`: some block is full in every draw.
All inputs are finite; a program needn't handle non-finite values.
Results may differ from the reference program's by a relative error of at most 0.004.
Values may be sent and summed in bfloat16 or wider, within the bound.
A program may use at most 128 MiB of HBM per device.

```python
import math
import jax
import jax.numpy as jnp
from jax import lax

STATE = 128
TOK_DEV = 512
HEADS = 128
CHANNELS = 8192
BLOCKS = 32
ITEM_COUNT_ALL = 16384
N_SEQ = 32


def draw_log_decay(key, part):
    key = jax.random.fold_in(key, 11)
    sampler_seeds = jax.random.split(key, 7)
    share = 0.5
    fast = jax.random.uniform(sampler_seeds[0], (HEADS,)) < share
    slow_rate = jnp.exp(jax.random.uniform(sampler_seeds[1], (HEADS,), jnp.float32, math.log(0.1), 0.0)) / ITEM_COUNT_ALL
    fast_rate = jnp.exp(jax.random.uniform(sampler_seeds[2], (HEADS,), jnp.float32, math.log(1.0 / 50.0), math.log(1.0 / 30.0)))
    expansion_factor = jnp.where(fast, fast_rate, slow_rate)
    items_within_tile = jnp.exp(jax.random.uniform(sampler_seeds[3], (HEADS, ITEM_COUNT_ALL // TOK_DEV), jnp.float32, math.log(0.5), math.log(2.0)))
    items_within_tile = jnp.repeat(items_within_tile, TOK_DEV, axis=1)
    span_jitter = jnp.exp(jax.random.uniform(sampler_seeds[4], (HEADS, ITEM_COUNT_ALL), jnp.float32, math.log(0.5), math.log(2.0)))
    offshoot_cluster = jax.random.uniform(sampler_seeds[5], (ITEM_COUNT_ALL,)) < 4.0 / ITEM_COUNT_ALL
    cluster_span = jax.random.uniform(sampler_seeds[6], (ITEM_COUNT_ALL,), jnp.float32, 0.22, 0.69)
    objective_value = expansion_factor[:, None] * items_within_tile * span_jitter + jnp.where(offshoot_cluster, cluster_span, 0.0)[None, :]
    return (-objective_value).astype(jnp.float32)


def draw_parents(key, part):
    key = jax.random.fold_in(key, 5)
    back = jax.random.randint(key, (BLOCKS,), 0, 4)
    index = jnp.arange(BLOCKS, dtype=jnp.int32)
    back = jnp.where(index == BLOCKS - 1, 0, back)
    parent = jnp.maximum(index - 1 - back, 0)
    return jnp.where(index == 0, -1, parent).astype(jnp.int32)


def draw_lengths(key, part):
    key = jax.random.fold_in(key, 7)
    first, second = jax.random.split(key)
    base = jax.random.randint(first, (BLOCKS,), TOK_DEV // 4, TOK_DEV + 1)
    full = jax.random.randint(second, (), 0, BLOCKS)
    index = jnp.arange(BLOCKS, dtype=jnp.int32)
    return jnp.where(index == full, TOK_DEV, base).astype(jnp.int32)


def steps_of(stream_key, dims, shards, least, top_value):
    level = 1.0
    for axis_at, blocks in shards:
        draws = jax.random.uniform(jax.random.fold_in(jax.random.fold_in(stream_key, 6), axis_at), (blocks,), jnp.float32, least / len(shards), top_value / len(shards))
        level = level * jnp.repeat(jnp.exp(draws), dims[axis_at] // blocks).reshape((-1,) + (1,) * (len(dims) - 1 - axis_at))
    return level


def noise(rng, extent, deviation, limit, cuts=(), kind=jnp.bfloat16):
    result = jax.random.normal(rng, extent, jnp.float32) * deviation
    if len(cuts) > 0:
        result = steps_of(rng, extent, cuts, -0.22, 0.18) * result
    return jnp.clip(result, min=-limit, max=limit).astype(kind)


def setup_inputs(seed: int = 0) -> dict:
    splits = jax.random.split(jax.random.key(seed), 8)
    x_in = noise(splits[0], (ITEM_COUNT_ALL, CHANNELS), 1.0, 6.0, ((0, 32), (1, 8)), jnp.float32)
    dy_out = noise(splits[1], (ITEM_COUNT_ALL, CHANNELS), 0.5, 3.0, ((0, 32), (1, 8)), jnp.float32)
    b_in = noise(splits[2], (ITEM_COUNT_ALL, STATE), 0.03, 0.18, ((0, 32),), jnp.float32)
    c_in = noise(splits[3], (ITEM_COUNT_ALL, STATE), 0.03, 0.18, ((0, 32),), jnp.float32)
    log_decay = draw_log_decay(jax.random.fold_in(splits[7], 71), 0)
    parents = draw_parents(jax.random.fold_in(splits[7], 71), 0)
    lengths = draw_lengths(jax.random.fold_in(splits[7], 71), 0)
    return {"x_in": x_in, "dy_out": dy_out, "b_in": b_in, "c_in": c_in, "log_decay": log_decay, "parents": parents, "lengths": lengths}


highest = lax.Precision.HIGHEST


def chain_weights(decays, parents, count):
    blocks = jnp.arange(count, dtype=jnp.int32)
    width_heads = decays.shape[1]

    def step(k, state):
        weights, coef, ancestor = state
        match = ancestor[:, None] == blocks[None, :]
        onehot = match.astype(jnp.float32)
        weights = weights + onehot[:, :, None] * coef[:, None, :]
        coef = coef * jnp.dot(onehot, decays, precision=highest)
        upward = jnp.sum(jnp.where(match, parents[None, :], 0), axis=1).astype(jnp.int32)
        ancestor = jnp.where(ancestor >= 0, upward, -1).astype(jnp.int32)
        return weights, coef, ancestor

    init = (jnp.zeros((count, count, width_heads), jnp.float32),
            jnp.ones((count, width_heads), jnp.float32),
            parents.astype(jnp.int32))
    weights, _, _ = lax.fori_loop(0, count, step, init)
    return weights


def local_states(x_blk, dy_blk, bmat, cmat, logd, length):
    rows = x_blk.shape[0]
    heads = logd.shape[0]
    width = x_blk.shape[1] // heads
    live = (jnp.arange(rows, dtype=jnp.int32) < length).astype(jnp.float32)
    xmask = x_blk * live[:, None]
    dymask = dy_blk * live[:, None]
    cumul = jnp.cumsum(logd * live[None, :], axis=1)
    last = cumul[:, -1]
    e_end = jnp.exp(last[:, None] - cumul)
    e_start = jnp.exp(cumul)
    xheads = xmask.reshape(rows, heads, width)
    dyheads = dymask.reshape(rows, heads, width)
    loc_end = jnp.einsum('tn,ht,thp->hnp', bmat, e_end, xheads, precision=highest)
    loc_adj = jnp.einsum('tn,ht,thp->hnp', cmat, e_start, dyheads, precision=highest)
    saved = (live, xheads, dyheads, cumul, e_end, e_start)
    return jnp.exp(last), loc_end.astype(jnp.bfloat16), loc_adj.astype(jnp.bfloat16), saved


def block_grads(bmat, cmat, saved, decay_tot, s_in, g_out):
    live, xheads, dyheads, cumul, e_end, e_start = saved
    rows = xheads.shape[0]
    heads = xheads.shape[1]
    scores = jnp.dot(cmat, bmat.T, precision=highest)
    steps = jnp.arange(rows, dtype=jnp.int32)
    lower = steps[:, None] >= steps[None, :]
    final = (steps == rows - 1).astype(jnp.float32)

    def one_head(carry, item):
        db_sum, dc_sum = carry
        xk, dk, ck, ee, es, dk_dec, hk, gk = item
        diff = jnp.where(lower, ck[:, None] - ck[None, :], 0.0)
        decay = jnp.where(lower, jnp.exp(diff), 0.0)
        pairs = jnp.dot(dk, xk.T, precision=highest)
        dsc = decay * scores
        dpr = decay * pairs
        joint = dsc * pairs
        bgo = jnp.dot(bmat, gk, precision=highest)
        chi = jnp.dot(cmat, hk, precision=highest)
        dx_head = (jnp.dot(dsc.T, dk, precision=highest) + ee[:, None] * bgo) * live[:, None]
        db_head = jnp.dot(dpr.T, cmat, precision=highest) + ee[:, None] * jnp.dot(xk, gk.T, precision=highest)
        dc_head = jnp.dot(dpr, bmat, precision=highest) + es[:, None] * jnp.dot(dk, hk.T, precision=highest)
        tail = ee * jnp.sum(bgo * xk, axis=1)
        extra = jnp.sum(tail) + dk_dec * jnp.sum(gk * hk)
        dcum = jnp.sum(joint, axis=1) - jnp.sum(joint, axis=0) + es * jnp.sum(chi * dk, axis=1) - tail + final * extra
        dlog = jnp.cumsum(dcum[::-1])[::-1] * live
        return (db_sum + db_head, dc_sum + dc_head), (dx_head, dlog)

    zero_n = jnp.zeros((rows, bmat.shape[1]), jnp.float32)
    items = (xheads.transpose(1, 0, 2), dyheads.transpose(1, 0, 2), cumul, e_end, e_start, decay_tot, s_in, g_out)
    (db_sum, dc_sum), (dx_all, dlog_all) = lax.scan(one_head, (zero_n, zero_n), items)
    dx = dx_all.transpose(1, 0, 2).reshape(rows, heads * xheads.shape[2])
    return dx, db_sum, dc_sum, dlog_all


def reference(x_in, dy_out, b_in, c_in, log_decay, parents, lengths):
    count = N_SEQ
    xs = x_in.reshape(count, TOK_DEV, CHANNELS)
    dys = dy_out.reshape(count, TOK_DEV, CHANNELS)
    bs = b_in.reshape(count, TOK_DEV, STATE)
    cs = c_in.reshape(count, TOK_DEV, STATE)
    logs = log_decay.reshape(HEADS, count, TOK_DEV).transpose(1, 0, 2)

    def first(item):
        xb, dyb, bb, cb, lb, ln = item
        decay_tot, loc_end, loc_adj, _ = local_states(xb, dyb, bb, cb, lb, ln)
        return decay_tot, loc_end, loc_adj

    decs, ends, adjs = lax.map(first, (xs, dys, bs, cs, logs, lengths))
    weights = chain_weights(decs, parents, count)
    s_in = jnp.einsum('bah,ahnp->bhnp', weights, ends.astype(jnp.float32), precision=highest)
    g_out = jnp.einsum('bah,bhnp->ahnp', weights, adjs.astype(jnp.float32), precision=highest)

    def second(item):
        xb, dyb, bb, cb, lb, ln, sb, gb = item
        decay_tot, _, _, saved = local_states(xb, dyb, bb, cb, lb, ln)
        return block_grads(bb, cb, saved, decay_tot, sb, gb)

    dx, db, dc, dlog = lax.map(second, (xs, dys, bs, cs, logs, lengths, s_in, g_out))
    x_grad = dx.reshape(ITEM_COUNT_ALL, CHANNELS)
    b_grad = db.reshape(ITEM_COUNT_ALL, STATE)
    c_grad = dc.reshape(ITEM_COUNT_ALL, STATE)
    decay_grad = dlog.transpose(1, 0, 2).reshape(HEADS, ITEM_COUNT_ALL)
    return x_grad, b_grad, c_grad, decay_grad
```

```python
import functools
import math

import jax
import jax.numpy as jnp
from jax import lax
from jax.experimental import pallas as pl
from jax.experimental.pallas import tpu as pltpu
from jax.sharding import PartitionSpec as P

f32 = jnp.float32
bf16 = jnp.bfloat16
MESH = pl.DeviceIdType.MESH
LOG2E = math.log2(math.e)

ROWS = 512
NST = 128
NH = 16
WID = 64
CH = NH * WID
TILE = 128
NT = ROWS // TILE
NY = 4
NZ = 8
NB = NY * NZ
QW = CH // NY
RW = NST // NZ
NMP = 8
SHARE = ROWS // NMP
CUT1, CUT2 = 3, 6
STEPS = 4
DZ_ORDER = (4, 3, 5, 2, 6, 1, 7, 0)


def dot(a, b):
    return jnp.dot(a, b, preferred_element_type=f32)


def dot_t(a, b):
    return lax.dot_general(a, b, (((1,), (1,)), ((), ())), preferred_element_type=f32)


def dot_0(a, b):
    return lax.dot_general(a, b, (((0,), (0,)), ((), ())), preferred_element_type=f32)


def split3(v):
    hi = v.astype(bf16)
    rest = v - hi.astype(f32)
    mid = rest.astype(bf16)
    low = (rest - mid.astype(f32)).astype(bf16)
    return hi, mid, low


def running(v, tri, reverse):
    tall = jnp.concatenate([v[:, TILE * i : TILE * (i + 1)] for i in range(NT)], axis=0)
    hi, mid, low = split3(tall)
    part = dot(hi, tri) + dot(mid, tri) + dot(low, tri)
    whole = jnp.sum(tall, axis=1, keepdims=True)
    pieces = [None] * NT
    carry = jnp.zeros((NH, 1), f32)
    order = range(NT - 1, -1, -1) if reverse else range(NT)
    for i in order:
        rows = slice(NH * i, NH * (i + 1))
        pieces[i] = part[rows] + carry
        carry = carry + whole[rows]
    return jnp.concatenate(pieces, axis=1)


def halves_of(v):
    hi = v.astype(bf16)
    return hi, (v - hi.astype(f32)).astype(bf16)


def kernel(
    lengths,
    prow,
    x_hbm,
    dy_hbm,
    b_ref,
    c_ref,
    logd_ref,
    xg_hbm,
    db_out,
    dc_out,
    dl_ref,
    x_v,
    dy_v,
    dx_v,
    eex_v,
    esdy_v,
    eexp_v,
    bt_v,
    ct_v,
    ccol_v,
    crow_v,
    last_v,
    st_v,
    mt_v,
    rowq_v,
    colq_v,
    tab_v,
    tab_s,
    send1,
    recv1,
    decx,
    decr,
    f_v,
    r_v,
    send2,
    recv2,
    part_v,
    rbuf,
    load_sem,
    out_sem,
    tab_sem,
    send_sem,
    recv_sem,
    own_sem,
):
    me = lax.axis_index("seq")
    mp = lax.axis_index("mp")
    my_y = lax.rem(me, NY)
    my_z = me // NY

    def group(i):
        return lax.rem(my_y + i, NY)

    def peer(i, dz):
        return lax.rem(my_z + dz, NZ) * NY + group(i)

    def lanes(q):
        return pl.ds(pl.multiple_of(q * QW, QW), QW)

    def to_seq(src, dst, j, k):
        pltpu.make_async_remote_copy(
            src_ref=src,
            dst_ref=dst,
            send_sem=send_sem.at[k],
            recv_sem=recv_sem.at[k],
            device_id={"seq": j},
            device_id_type=MESH,
        ).start()

    def to_mp(src, dst, j, k):
        pltpu.make_async_remote_copy(
            src_ref=src,
            dst_ref=dst,
            send_sem=send_sem.at[k],
            recv_sem=recv_sem.at[k],
            device_id={"mp": j},
            device_id_type=MESH,
        ).start()

    def settle(like, sem):
        pltpu.make_async_copy(like, like, sem).wait()

    loads = []
    for ref, buf, base in ((x_hbm, x_v, 0), (dy_hbm, dy_v, NY)):
        for i in range(NY):
            q = group(i)
            load = pltpu.make_async_copy(ref.at[:, lanes(q)], buf.at[:, lanes(q)], load_sem.at[base + i])
            load.start()
            loads.append(load)

    barrier = pltpu.get_barrier_semaphore()
    for i in range(NY):
        for dz in DZ_ORDER:
            if i or dz:
                pl.semaphore_signal(barrier, inc=1, device_id={"seq": peer(i, dz)}, device_id_type=MESH)
    for k in range(1, NMP):
        pl.semaphore_signal(barrier, inc=1, device_id={"mp": lax.rem(mp + k, NMP)}, device_id_type=MESH)

    length = lengths[me]

    ti = lax.broadcasted_iota(jnp.int32, (TILE, TILE), 0)
    tj = lax.broadcasted_iota(jnp.int32, (TILE, TILE), 1)
    upto = jnp.where(ti <= tj, 1.0, 0.0).astype(bf16)
    lane = lax.broadcasted_iota(jnp.int32, (NH, ROWS), 1)
    live = lane < length
    logd = jnp.where(live, logd_ref[...] * LOG2E, 0.0)
    cum = running(logd, upto, False)
    last = cum[:, ROWS - 1 : ROWS]
    last_v[...] = jnp.broadcast_to(last, (NH, TILE))
    ee = jnp.where(live, jnp.exp2(last - cum), 0.0)
    es = jnp.exp2(cum)
    ee_hi = ee.astype(bf16).astype(f32)
    es_hi = es.astype(bf16).astype(f32)
    stack = jnp.concatenate(
        [ee_hi, ee - ee_hi, es_hi, es - es_hi, cum, jnp.zeros((NST - 5 * NH, ROWS), f32)], axis=0
    )
    cols = stack.T
    cols_b = cols.astype(bf16)
    bt_hi, bt_lo = halves_of(b_ref[...].T)
    bt_v[0] = bt_hi
    bt_v[1] = bt_lo

    er = lax.broadcasted_iota(jnp.int32, (NST, QW), 0)
    eh = lax.broadcasted_iota(jnp.int32, (NST, QW), 1) // WID

    def spread(q, base, rows=cols_b):
        head = eh + (q * (NH // NY) + base)
        return dot(rows, jnp.where((er == head) | (er == head + NH), 1.0, 0.0).astype(bf16))

    def state_of(t_v, wide):
        hi, low = halves_of(wide)
        total = dot(t_v[0], hi) + dot(t_v[1], hi) + dot(t_v[0], low)
        return hi, total.astype(bf16)

    for i in range(NY):
        q = group(i)
        e_wide = spread(q, 0)
        eexp_v[:, lanes(q)] = e_wide
        loads[i].wait()
        hi, loc = state_of(bt_v, x_v[:, lanes(q)] * e_wide)
        eex_v[:, lanes(q)] = hi
        decx[q] = spread(q, 2 * NH, cols_b[ROWS - RW :, :])[RW - 1 :, :]
        for r in range(NZ):
            send1[0, r * NY + q] = loc[RW * r : RW * (r + 1), :]
        if i == 0:
            pl.semaphore_wait(barrier, NB - 1 + NMP - 1)
        for dz in DZ_ORDER:
            if i or dz:
                j = peer(i, dz)
                to_seq(send1.at[0, j], recv1.at[0, me], j, 0)
        for dz in DZ_ORDER:
            if i or dz:
                j = peer(i, dz)
                to_seq(decx.at[q], decr.at[me], j, 2)

    ct_hi, ct_lo = halves_of(c_ref[...].T)
    ct_v[0] = ct_hi
    ct_v[1] = ct_lo
    row_live = lax.broadcasted_iota(jnp.int32, (ROWS, QW), 0) < length
    for i in range(NY):
        q = group(i)
        s_wide = spread(q, 2 * NH)
        loads[NY + i].wait()
        dy = jnp.where(row_live, dy_v[:, lanes(q)], 0.0)
        dy_v[:, lanes(q)] = dy
        hi, loc = state_of(ct_v, dy * s_wide)
        esdy_v[:, lanes(q)] = hi
        for r in range(NZ):
            send1[1, r * NY + q] = loc[RW * r : RW * (r + 1), :]
        for dz in DZ_ORDER:
            if i or dz:
                j = peer(i, dz)
                to_seq(send1.at[1, j], recv1.at[1, me], j, 1)
    own = [
        pltpu.make_async_copy(send1.at[0, me], recv1.at[0, me], own_sem.at[0]),
        pltpu.make_async_copy(send1.at[1, me], recv1.at[1, me], own_sem.at[1]),
        pltpu.make_async_copy(decx.at[my_y], decr.at[me], own_sem.at[2]),
    ]
    for copy in own:
        copy.start()

    bi = lax.broadcasted_iota(jnp.int32, (NB, NB), 0)
    bj = lax.broadcasted_iota(jnp.int32, (NB, NB), 1)
    par = jnp.broadcast_to(prow[...], (NB, NB))
    par_col = jnp.sum(jnp.where(bi == bj, par, 0), axis=1, keepdims=True)
    first = jnp.min(jnp.where(par == bi, bj, NB), axis=1, keepdims=True)
    sibling = jnp.min(jnp.where((par == par_col) & (bj > bi), bj, NB), axis=1, keepdims=True)
    tl = lax.broadcasted_iota(jnp.int32, (NB, TILE), 1)
    tab_v[...] = jnp.where(
        tl == 0, first, jnp.where(tl == 1, sibling, jnp.where(par_col < 0, NB, par_col))
    )
    tab = pltpu.make_async_copy(tab_v, tab_s, tab_sem)
    tab.start()

    st_v[...] = lax.dot_general(
        b_ref[...],
        c_ref[...],
        (((1,), (1,)), ((), ())),
        preferred_element_type=f32,
        precision=lax.Precision.HIGHEST,
    )
    mt_v[...] = jnp.zeros_like(mt_v)
    colq_v[...] = jnp.zeros_like(colq_v)
    for h in range(NH):
        crow_v[h] = cum[h : h + 1, :]
        ccol_v[h] = jnp.broadcast_to(cols[:, 4 * NH + h : 4 * NH + h + 1], (ROWS, TILE))
    left = lax.broadcasted_iota(jnp.int32, (ROWS, TILE), 1) < WID
    nil = jnp.zeros((ROWS, TILE), bf16)

    def pair(k, carry):
        span = pl.ds(pl.multiple_of(k * TILE, TILE), TILE)
        xk = x_v[:, span]
        dk = dy_v[:, span]
        xr = pltpu.roll(xk, WID, 1)
        dr = pltpu.roll(dk, WID, 1)
        xs, ds = [], []
        for s in range(2):
            hi, low = halves_of(jnp.where(left, xk, xr) if s == 0 else jnp.where(left, xr, xk))
            both = jnp.where(left, hi, low)
            xs.append(jnp.concatenate([both, both], axis=1))
            ds.append(halves_of(jnp.where(left, dk, dr) if s == 0 else jnp.where(left, dr, dk)))
        dg = [jnp.concatenate(d, axis=1) for d in ds]
        dn = [jnp.where(left, ds[0][0], nil), jnp.where(left, nil, ds[1][0])]
        dx = [jnp.zeros((TILE, TILE), f32) for _ in range(NT)]
        rowq = [[None] * NT, [None] * NT]
        colq = [[None] * NT, [None] * NT]
        for ib in range(NT):
            ts = slice(TILE * ib, TILE * (ib + 1))
            dt = jnp.concatenate([dn[0][ts, :], dn[1][ts, :]], axis=0)
            for jb in range(ib + 1):
                us = slice(TILE * jb, TILE * (jb + 1))
                score = st_v[us, ts]
                total = mt_v[us, ts]
                wide = []
                for s in range(2):
                    h = 2 * k + s
                    g = dot_t(xs[s][us, :], dg[s][ts, :])
                    diff = crow_v[h, :, ts] - ccol_v[h, us, :]
                    if ib == jb:
                        diff = jnp.where(tj >= ti, diff, -1e30)
                    e = jnp.exp2(diff)
                    dsc = e * score
                    total = total + e * g
                    wide.append(dsc.astype(bf16))
                    joint = dsc * g
                    down = jnp.sum(joint, axis=0, keepdims=True)
                    rowq[s][ib] = down if jb == 0 else rowq[s][ib] + down
                    colq[s][jb] = joint if ib == jb else colq[s][jb] + joint
                mt_v[us, ts] = total
                dx[jb] = dx[jb] + dot(jnp.concatenate(wide, axis=1), dt)
        for s in range(2):
            rowq_v[2 * k + s] = jnp.concatenate(rowq[s], axis=1)
        for jb in range(NT):
            us = slice(TILE * jb, TILE * (jb + 1))
            both = colq_v[us, :]
            for s in range(2):
                tot = jnp.sum(colq[s][jb], axis=1, keepdims=True)
                both = jnp.where(tj == 2 * NH + 2 * k + s, tot, both)
            colq_v[us, :] = both
            dx_v[us, span] = dx[jb]
        return carry

    lax.fori_loop(0, CUT1, pair, 0)

    tab.wait()
    for copy in own:
        copy.wait()
    f_v[NB] = jnp.zeros((RW, QW), f32)
    r_v[NB] = jnp.zeros((RW, QW), f32)
    settle(recv1.at[0, pl.ds(0, NB - 1)], recv_sem.at[0])
    settle(decr.at[pl.ds(0, NB - 1)], recv_sem.at[2])

    def forward(b, carry):
        state = f_v[tab_s[b, 2]]
        send2[0, b] = state.astype(bf16)
        f_v[b] = recv1[0, b].astype(f32) + decr[b] * state
        return carry

    def backward(k, carry):
        a = NB - 1 - k
        adj = r_v[tab_s[a, 0]]
        send2[1, a] = adj.astype(bf16)
        r_v[a] = recv1[1, a].astype(f32) + decr[a] * adj + r_v[tab_s[a, 1]]
        return carry

    def hand_back(w, k):
        for dz in DZ_ORDER:
            for i in range(NY):
                if i or dz:
                    j = peer(i, dz)
                    to_seq(send2.at[w, j], recv2.at[w, me], j, k)
        copy = pltpu.make_async_copy(send2.at[w, me], recv2.at[w, me], own_sem.at[3 + w])
        copy.start()
        return copy

    lax.fori_loop(0, NB, forward, 0)
    own_s = hand_back(0, 3)

    lax.fori_loop(CUT1, CUT2, pair, 0)

    settle(recv1.at[1, pl.ds(0, NB - 1)], recv_sem.at[1])
    lax.fori_loop(0, NB, backward, 0)
    own_g = hand_back(1, 4)

    lax.fori_loop(CUT2, NH // 2, pair, 0)

    b_hi, b_lo = halves_of(b_ref[...])
    c_hi, c_lo = halves_of(c_ref[...])
    mt_hi, mt_lo = halves_of(mt_v[...])
    db = dot(mt_hi, c_hi) + dot(mt_lo, c_hi) + dot(mt_hi, c_lo)
    dc = dot_0(mt_hi, b_hi) + dot_0(mt_lo, b_hi) + dot_0(mt_hi, b_lo)
    b_two = jnp.concatenate([b_hi, b_lo], axis=1)
    c_two = jnp.concatenate([c_hi, c_lo], axis=1)

    def arrived(w, q):
        return jnp.concatenate([recv2[w, r * NY + q] for r in range(NZ)], axis=0)

    def scatter(w, terms, k):
        part_v[w] = terms.astype(bf16)
        for d in (4, 3, 5, 2, 6, 1, 7):
            to = lax.rem(mp + d, NMP)
            to_mp(part_v.at[w, share_of(to)], rbuf.at[w, mp], to, k)
        copy = pltpu.make_async_copy(part_v.at[w, share_of(mp)], rbuf.at[w, mp], own_sem.at[5 + w])
        copy.start()
        return copy

    def share_of(k):
        return pl.ds(pl.multiple_of(k * SHARE, SHARE), SHARE)

    def spread_share(w, out, own_part, k):
        own_part.wait()
        settle(rbuf.at[w, pl.ds(0, NMP - 1)], recv_sem.at[k])
        share = rbuf[w, 0].astype(f32)
        for d in range(1, NMP):
            share = share + rbuf[w, d].astype(f32)
        out[share_of(mp), :] = share.astype(bf16)
        for d in (4, 3, 5, 2, 6, 1, 7):
            to_mp(out.at[share_of(mp), :], out.at[share_of(mp), :], lax.rem(mp + d, NMP), k + 1)

    own_s.wait()
    settle(recv2.at[0, pl.ds(0, NB - 1)], recv_sem.at[3])
    s_in = [arrived(0, q) for q in range(NY)]
    for q in range(NY):
        dc = dc + dot_t(esdy_v[:, QW * q : QW * (q + 1)], s_in[q])
    own_dc = scatter(0, dc, 5)
    acc = colq_v[...]
    sel_r = lax.broadcasted_iota(jnp.int32, (QW, TILE), 0) // WID
    sel_l = lax.broadcasted_iota(jnp.int32, (QW, TILE), 1)

    def picks(q, base):
        return jnp.where(sel_l == sel_r + (q * (NH // NY) + base), 1.0, 0.0).astype(bf16)

    for q in range(NY):
        chi = dot(c_two, jnp.concatenate([s_in[q], s_in[q]], axis=0))
        head = chi * esdy_v[:, QW * q : QW * (q + 1)].astype(f32)
        acc = acc + dot(head.astype(bf16), picks(q, 0))
    spread_share(0, dc_out, own_dc, 5)

    own_g.wait()
    settle(recv2.at[1, pl.ds(0, NB - 1)], recv_sem.at[4])
    g_out = [arrived(1, q) for q in range(NY)]
    for q in range(NY):
        db = db + dot_t(eex_v[:, QW * q : QW * (q + 1)], g_out[q])
    own_db = scatter(1, db, 7)

    gs = jnp.zeros((8, NST), f32)
    stores = []
    for q in range(NY):
        span = slice(QW * q, QW * (q + 1))
        bgo = dot(b_two, jnp.concatenate([g_out[q], g_out[q]], axis=0))
        dx_b = (dx_v[:, span] + eexp_v[:, span] * bgo).astype(bf16)
        eex = eex_v[:, span].astype(f32)
        esdy_v[:, span] = dx_b
        out = pltpu.make_async_copy(esdy_v.at[:, span], xg_hbm.at[:, span], out_sem.at[q])
        out.start()
        stores.append(out)
        acc = acc + dot((bgo * eex).astype(bf16), picks(q, NH))
        both = jnp.sum(g_out[q].astype(f32) * s_in[q].astype(f32), axis=0, keepdims=True)
        both_hi, both_lo = halves_of(jnp.broadcast_to(both, (8, QW)))
        gs = gs + dot(both_hi, picks(q, 0)) + dot(both_lo, picks(q, 0))
    flat = acc.T
    gs_col = gs.T[0:NH, 0:1]
    head = flat[0:NH]
    tail = flat[NH : 2 * NH]
    colq = flat[2 * NH : 3 * NH]
    since = jnp.where(ti >= tj, 1.0, 0.0).astype(bf16)
    before = jnp.where(ti < tj, 1.0, 0.0).astype(bf16)
    dec = jnp.exp2(last_v[:, 0:1])
    rowq = jnp.concatenate([rowq_v[h] for h in range(NH)], axis=0)
    total = running(rowq - colq + head, since, True) + running(tail, before, False) + dec * gs_col
    dl_ref[...] = jnp.where(live, total, 0.0)

    spread_share(1, db_out, own_db, 7)

    settle(send1.at[0, pl.ds(0, NB - 1)], send_sem.at[0])
    settle(send1.at[1, pl.ds(0, NB - 1)], send_sem.at[1])
    settle(decr.at[pl.ds(0, NB - 1)], send_sem.at[2])
    settle(send2.at[0, pl.ds(0, NB - 1)], send_sem.at[3])
    settle(send2.at[1, pl.ds(0, NB - 1)], send_sem.at[4])
    for w in range(2):
        settle(rbuf.at[w, pl.ds(0, NMP - 1)], send_sem.at[5 + 2 * w])
        settle(rbuf.at[w, pl.ds(0, NMP - 1)], send_sem.at[6 + 2 * w])
    for out in stores:
        out.wait()
    settle(rbuf.at[0, pl.ds(0, NMP - 1)], recv_sem.at[6])
    settle(rbuf.at[1, pl.ds(0, NMP - 1)], recv_sem.at[8])


def finish(xg_ref, db_ref, dc_ref, dl_ref, xg_out, db_out, dc_out, dl_out):
    xg_out[...] = xg_ref[...].astype(f32)

    @pl.when(pl.program_id(0) == 0)
    def _():
        db_out[...] = db_ref[...].astype(f32)
        dc_out[...] = dc_ref[...].astype(f32)
        dl_out[...] = dl_ref[...]


def on_device(x_in, dy_out, b_in, c_in, log_decay, parents, lengths):
    vmem = pl.BlockSpec(memory_space=pltpu.VMEM)
    smem = pl.BlockSpec(memory_space=pltpu.SMEM)
    anywhere = pl.BlockSpec(memory_space=pl.ANY)
    wide = (ROWS, CH)
    dma = pltpu.SemaphoreType.DMA
    given = pl.pallas_call(
        kernel,
        out_shape=(
            jax.ShapeDtypeStruct(wide, bf16),
            jax.ShapeDtypeStruct((ROWS, NST), bf16),
            jax.ShapeDtypeStruct((ROWS, NST), bf16),
            jax.ShapeDtypeStruct((NH, ROWS), f32),
        ),
        in_specs=[smem, vmem, anywhere, anywhere, vmem, vmem, vmem],
        out_specs=(anywhere, vmem, vmem, vmem),
        scratch_shapes=[
            pltpu.VMEM(wide, f32),
            pltpu.VMEM(wide, f32),
            pltpu.VMEM(wide, f32),
            pltpu.VMEM(wide, bf16),
            pltpu.VMEM(wide, bf16),
            pltpu.VMEM(wide, f32),
            pltpu.VMEM((2, NST, ROWS), bf16),
            pltpu.VMEM((2, NST, ROWS), bf16),
            pltpu.VMEM((NH, ROWS, TILE), f32),
            pltpu.VMEM((NH, 1, ROWS), f32),
            pltpu.VMEM((NH, TILE), f32),
            pltpu.VMEM((ROWS, ROWS), f32),
            pltpu.VMEM((ROWS, ROWS), f32),
            pltpu.VMEM((NH, 1, ROWS), f32),
            pltpu.VMEM((ROWS, TILE), f32),
            pltpu.VMEM((NB, TILE), jnp.int32),
            pltpu.SMEM((NB, TILE), jnp.int32),
            pltpu.VMEM((2, NB, RW, QW), bf16),
            pltpu.VMEM((2, NB, RW, QW), bf16),
            pltpu.VMEM((NY, 1, QW), f32),
            pltpu.VMEM((NB, 1, QW), f32),
            pltpu.VMEM((NB + 1, RW, QW), f32),
            pltpu.VMEM((NB + 1, RW, QW), f32),
            pltpu.VMEM((2, NB, RW, QW), bf16),
            pltpu.VMEM((2, NB, RW, QW), bf16),
            pltpu.VMEM((2, ROWS, NST), bf16),
            pltpu.VMEM((2, NMP, SHARE, NST), bf16),
            dma((2 * NY,)),
            dma((NY,)),
            dma,
            dma((9,)),
            dma((9,)),
            dma((7,)),
        ],
        compiler_params=pltpu.CompilerParams(
            collective_id=0, has_side_effects=True, vmem_limit_bytes=56 * 1024 * 1024
        ),
    )(lengths, parents.reshape(1, NB), x_in, dy_out, b_in, c_in, log_decay)
    step = ROWS // STEPS
    rows = pl.BlockSpec((step, CH), lambda i: (i, 0))
    whole = pl.BlockSpec((ROWS, NST), lambda i: (0, 0))
    decays = pl.BlockSpec((NH, ROWS), lambda i: (0, 0))
    return tuple(
        pl.pallas_call(
            finish,
            grid=(STEPS,),
            out_shape=(
                jax.ShapeDtypeStruct(wide, f32),
                jax.ShapeDtypeStruct((ROWS, NST), f32),
                jax.ShapeDtypeStruct((ROWS, NST), f32),
                jax.ShapeDtypeStruct((NH, ROWS), f32),
            ),
            in_specs=[rows, whole, whole, decays],
            out_specs=(rows, whole, whole, decays),
        )(*given)
    )


def solution(mesh):
    return jax.shard_map(
        on_device,
        mesh=mesh,
        in_specs=(
            P("seq", "mp"),
            P("seq", "mp"),
            P("seq", None),
            P("seq", None),
            P("mp", "seq"),
            P(),
            P(),
        ),
        out_specs=(P("seq", "mp"), P("seq", None), P("seq", None), P("mp", "seq")),
        check_vma=False,
    )
```

```python
import functools
import math

import jax
import jax.numpy as jnp
from jax import lax
from jax.experimental import pallas as pl
from jax.experimental.pallas import tpu as pltpu
from jax.sharding import PartitionSpec as P

f32 = jnp.float32
bf16 = jnp.bfloat16
MESH = pl.DeviceIdType.MESH
LOG2E = math.log2(math.e)

ROWS = 512
NST = 128
NH = 16
WID = 64
CH = NH * WID
TILE = 128
NT = ROWS // TILE
NY = 4
NZ = 8
NB = NY * NZ
QW = CH // NY
RW = NST // NZ
NMP = 8
SHARE = ROWS // NMP
CUT1, CUT2 = 3, 6
DZ_ORDER = (4, 3, 5, 2, 6, 1, 7, 0)


def dot(a, b):
    return jnp.dot(a, b, preferred_element_type=f32)


def dot_t(a, b):
    return lax.dot_general(a, b, (((1,), (1,)), ((), ())), preferred_element_type=f32)


def dot_0(a, b):
    return lax.dot_general(a, b, (((0,), (0,)), ((), ())), preferred_element_type=f32)


def split3(v):
    hi = v.astype(bf16)
    rest = v - hi.astype(f32)
    mid = rest.astype(bf16)
    low = (rest - mid.astype(f32)).astype(bf16)
    return hi, mid, low


def running(v, tri, reverse):
    tall = jnp.concatenate([v[:, TILE * i : TILE * (i + 1)] for i in range(NT)], axis=0)
    hi, mid, low = split3(tall)
    part = dot(hi, tri) + dot(mid, tri) + dot(low, tri)
    whole = jnp.sum(tall, axis=1, keepdims=True)
    pieces = [None] * NT
    carry = jnp.zeros((NH, 1), f32)
    order = range(NT - 1, -1, -1) if reverse else range(NT)
    for i in order:
        rows = slice(NH * i, NH * (i + 1))
        pieces[i] = part[rows] + carry
        carry = carry + whole[rows]
    return jnp.concatenate(pieces, axis=1)


def halves_of(v):
    hi = v.astype(bf16)
    return hi, (v - hi.astype(f32)).astype(bf16)


def kernel(
    lengths,
    prow,
    x_hbm,
    dy_hbm,
    b_ref,
    c_ref,
    logd_ref,
    dx_v,
    db_out,
    dc_out,
    dl_ref,
    x_v,
    dy_v,
    eex_v,
    esdy_v,
    eexp_v,
    bt_v,
    ct_v,
    ccol_v,
    crow_v,
    last_v,
    st_v,
    mt_v,
    rowq_v,
    colq_v,
    tab_v,
    tab_s,
    send1,
    recv1,
    decx,
    decr,
    f_v,
    r_v,
    send2,
    recv2,
    part_v,
    rbuf,
    load_sem,
    tab_sem,
    send_sem,
    recv_sem,
    own_sem,
):
    me = lax.axis_index("seq")
    mp = lax.axis_index("mp")
    my_y = lax.rem(me, NY)
    my_z = me // NY

    def group(i):
        return lax.rem(my_y + i, NY)

    def peer(i, dz):
        return lax.rem(my_z + dz, NZ) * NY + group(i)

    def lanes(q):
        return pl.ds(pl.multiple_of(q * QW, QW), QW)

    def to_seq(src, dst, j, k):
        pltpu.make_async_remote_copy(
            src_ref=src,
            dst_ref=dst,
            send_sem=send_sem.at[k],
            recv_sem=recv_sem.at[k],
            device_id={"seq": j},
            device_id_type=MESH,
        ).start()

    def to_mp(src, dst, j, k):
        pltpu.make_async_remote_copy(
            src_ref=src,
            dst_ref=dst,
            send_sem=send_sem.at[k],
            recv_sem=recv_sem.at[k],
            device_id={"mp": j},
            device_id_type=MESH,
        ).start()

    def settle(like, sem):
        pltpu.make_async_copy(like, like, sem).wait()

    loads = []
    for ref, buf, base in ((x_hbm, x_v, 0), (dy_hbm, dy_v, NY)):
        for i in range(NY):
            q = group(i)
            load = pltpu.make_async_copy(ref.at[:, lanes(q)], buf.at[:, lanes(q)], load_sem.at[base + i])
            load.start()
            loads.append(load)

    barrier = pltpu.get_barrier_semaphore()
    for i in range(NY):
        for dz in DZ_ORDER:
            if i or dz:
                pl.semaphore_signal(barrier, inc=1, device_id={"seq": peer(i, dz)}, device_id_type=MESH)
    for k in range(1, NMP):
        pl.semaphore_signal(barrier, inc=1, device_id={"mp": lax.rem(mp + k, NMP)}, device_id_type=MESH)

    length = lengths[me]

    ti = lax.broadcasted_iota(jnp.int32, (TILE, TILE), 0)
    tj = lax.broadcasted_iota(jnp.int32, (TILE, TILE), 1)
    upto = jnp.where(ti <= tj, 1.0, 0.0).astype(bf16)
    lane = lax.broadcasted_iota(jnp.int32, (NH, ROWS), 1)
    live = lane < length
    logd = jnp.where(live, logd_ref[...] * LOG2E, 0.0)
    cum = running(logd, upto, False)
    last = cum[:, ROWS - 1 : ROWS]
    last_v[...] = jnp.broadcast_to(last, (NH, TILE))
    ee = jnp.where(live, jnp.exp2(last - cum), 0.0)
    es = jnp.exp2(cum)
    ee_hi = ee.astype(bf16).astype(f32)
    es_hi = es.astype(bf16).astype(f32)
    stack = jnp.concatenate(
        [ee_hi, ee - ee_hi, es_hi, es - es_hi, cum, jnp.zeros((NST - 5 * NH, ROWS), f32)], axis=0
    )
    cols = stack.T
    cols_b = cols.astype(bf16)
    bt_hi, bt_lo = halves_of(b_ref[...].T)
    bt_v[0] = bt_hi
    bt_v[1] = bt_lo

    er = lax.broadcasted_iota(jnp.int32, (NST, QW), 0)
    eh = lax.broadcasted_iota(jnp.int32, (NST, QW), 1) // WID

    def spread(q, base, rows=cols_b):
        head = eh + (q * (NH // NY) + base)
        return dot(rows, jnp.where((er == head) | (er == head + NH), 1.0, 0.0).astype(bf16))

    def state_of(t_v, wide):
        hi, low = halves_of(wide)
        total = dot(t_v[0], hi) + dot(t_v[1], hi) + dot(t_v[0], low)
        return hi, total.astype(bf16)

    for i in range(NY):
        q = group(i)
        e_wide = spread(q, 0)
        eexp_v[:, lanes(q)] = e_wide
        loads[i].wait()
        hi, loc = state_of(bt_v, x_v[:, lanes(q)] * e_wide)
        eex_v[:, lanes(q)] = hi
        decx[q] = spread(q, 2 * NH, cols_b[ROWS - RW :, :])[RW - 1 :, :]
        for r in range(NZ):
            send1[0, r * NY + q] = loc[RW * r : RW * (r + 1), :]
        if i == 0:
            pl.semaphore_wait(barrier, NB - 1 + NMP - 1)
        for dz in DZ_ORDER:
            if i or dz:
                j = peer(i, dz)
                to_seq(send1.at[0, j], recv1.at[0, me], j, 0)
        for dz in DZ_ORDER:
            if i or dz:
                j = peer(i, dz)
                to_seq(decx.at[q], decr.at[me], j, 2)

    ct_hi, ct_lo = halves_of(c_ref[...].T)
    ct_v[0] = ct_hi
    ct_v[1] = ct_lo
    row_live = lax.broadcasted_iota(jnp.int32, (ROWS, QW), 0) < length
    for i in range(NY):
        q = group(i)
        s_wide = spread(q, 2 * NH)
        loads[NY + i].wait()
        dy = jnp.where(row_live, dy_v[:, lanes(q)], 0.0)
        dy_v[:, lanes(q)] = dy
        hi, loc = state_of(ct_v, dy * s_wide)
        esdy_v[:, lanes(q)] = hi
        for r in range(NZ):
            send1[1, r * NY + q] = loc[RW * r : RW * (r + 1), :]
        for dz in DZ_ORDER:
            if i or dz:
                j = peer(i, dz)
                to_seq(send1.at[1, j], recv1.at[1, me], j, 1)
    own = [
        pltpu.make_async_copy(send1.at[0, me], recv1.at[0, me], own_sem.at[0]),
        pltpu.make_async_copy(send1.at[1, me], recv1.at[1, me], own_sem.at[1]),
        pltpu.make_async_copy(decx.at[my_y], decr.at[me], own_sem.at[2]),
    ]
    for copy in own:
        copy.start()

    bi = lax.broadcasted_iota(jnp.int32, (NB, NB), 0)
    bj = lax.broadcasted_iota(jnp.int32, (NB, NB), 1)
    par = jnp.broadcast_to(prow[...], (NB, NB))
    par_col = jnp.sum(jnp.where(bi == bj, par, 0), axis=1, keepdims=True)
    first = jnp.min(jnp.where(par == bi, bj, NB), axis=1, keepdims=True)
    sibling = jnp.min(jnp.where((par == par_col) & (bj > bi), bj, NB), axis=1, keepdims=True)
    tl = lax.broadcasted_iota(jnp.int32, (NB, TILE), 1)
    tab_v[...] = jnp.where(
        tl == 0, first, jnp.where(tl == 1, sibling, jnp.where(par_col < 0, NB, par_col))
    )
    tab = pltpu.make_async_copy(tab_v, tab_s, tab_sem)
    tab.start()

    st_v[...] = lax.dot_general(
        b_ref[...],
        c_ref[...],
        (((1,), (1,)), ((), ())),
        preferred_element_type=f32,
        precision=lax.Precision.HIGHEST,
    )
    mt_v[...] = jnp.zeros_like(mt_v)
    colq_v[...] = jnp.zeros_like(colq_v)
    for h in range(NH):
        crow_v[h] = cum[h : h + 1, :]
        ccol_v[h] = jnp.broadcast_to(cols[:, 4 * NH + h : 4 * NH + h + 1], (ROWS, TILE))
    left = lax.broadcasted_iota(jnp.int32, (ROWS, TILE), 1) < WID
    nil = jnp.zeros((ROWS, TILE), bf16)

    def pair(k, carry):
        span = pl.ds(pl.multiple_of(k * TILE, TILE), TILE)
        xk = x_v[:, span]
        dk = dy_v[:, span]
        xr = pltpu.roll(xk, WID, 1)
        dr = pltpu.roll(dk, WID, 1)
        xs, ds = [], []
        for s in range(2):
            hi, low = halves_of(jnp.where(left, xk, xr) if s == 0 else jnp.where(left, xr, xk))
            both = jnp.where(left, hi, low)
            xs.append(jnp.concatenate([both, both], axis=1))
            ds.append(halves_of(jnp.where(left, dk, dr) if s == 0 else jnp.where(left, dr, dk)))
        dg = [jnp.concatenate(d, axis=1) for d in ds]
        dn = [jnp.where(left, ds[0][0], nil), jnp.where(left, nil, ds[1][0])]
        dx = [jnp.zeros((TILE, TILE), f32) for _ in range(NT)]
        rowq = [[None] * NT, [None] * NT]
        colq = [[None] * NT, [None] * NT]
        for ib in range(NT):
            ts = slice(TILE * ib, TILE * (ib + 1))
            dt = jnp.concatenate([dn[0][ts, :], dn[1][ts, :]], axis=0)
            for jb in range(ib + 1):
                us = slice(TILE * jb, TILE * (jb + 1))
                score = st_v[us, ts]
                total = mt_v[us, ts]
                wide = []
                for s in range(2):
                    h = 2 * k + s
                    g = dot_t(xs[s][us, :], dg[s][ts, :])
                    diff = crow_v[h, :, ts] - ccol_v[h, us, :]
                    if ib == jb:
                        diff = jnp.where(tj >= ti, diff, -1e30)
                    e = jnp.exp2(diff)
                    dsc = e * score
                    total = total + e * g
                    wide.append(dsc.astype(bf16))
                    joint = dsc * g
                    down = jnp.sum(joint, axis=0, keepdims=True)
                    rowq[s][ib] = down if jb == 0 else rowq[s][ib] + down
                    colq[s][jb] = joint if ib == jb else colq[s][jb] + joint
                mt_v[us, ts] = total
                dx[jb] = dx[jb] + dot(jnp.concatenate(wide, axis=1), dt)
        for s in range(2):
            rowq_v[2 * k + s] = jnp.concatenate(rowq[s], axis=1)
        for jb in range(NT):
            us = slice(TILE * jb, TILE * (jb + 1))
            both = colq_v[us, :]
            for s in range(2):
                tot = jnp.sum(colq[s][jb], axis=1, keepdims=True)
                both = jnp.where(tj == 2 * NH + 2 * k + s, tot, both)
            colq_v[us, :] = both
            dx_v[us, span] = dx[jb]
        return carry

    lax.fori_loop(0, CUT1, pair, 0)

    tab.wait()
    for copy in own:
        copy.wait()
    f_v[NB] = jnp.zeros((RW, QW), f32)
    r_v[NB] = jnp.zeros((RW, QW), f32)
    settle(recv1.at[0, pl.ds(0, NB - 1)], recv_sem.at[0])
    settle(decr.at[pl.ds(0, NB - 1)], recv_sem.at[2])

    def forward(b, carry):
        state = f_v[tab_s[b, 2]]
        send2[0, b] = state.astype(bf16)
        f_v[b] = recv1[0, b].astype(f32) + decr[b] * state
        return carry

    def backward(k, carry):
        a = NB - 1 - k
        adj = r_v[tab_s[a, 0]]
        send2[1, a] = adj.astype(bf16)
        r_v[a] = recv1[1, a].astype(f32) + decr[a] * adj + r_v[tab_s[a, 1]]
        return carry

    def hand_back(w, k):
        for dz in DZ_ORDER:
            for i in range(NY):
                if i or dz:
                    j = peer(i, dz)
                    to_seq(send2.at[w, j], recv2.at[w, me], j, k)
        copy = pltpu.make_async_copy(send2.at[w, me], recv2.at[w, me], own_sem.at[3 + w])
        copy.start()
        return copy

    lax.fori_loop(0, NB, forward, 0)
    own_s = hand_back(0, 3)

    lax.fori_loop(CUT1, CUT2, pair, 0)

    settle(recv1.at[1, pl.ds(0, NB - 1)], recv_sem.at[1])
    lax.fori_loop(0, NB, backward, 0)
    own_g = hand_back(1, 4)

    lax.fori_loop(CUT2, NH // 2, pair, 0)

    b_hi, b_lo = halves_of(b_ref[...])
    c_hi, c_lo = halves_of(c_ref[...])
    mt_hi, mt_lo = halves_of(mt_v[...])
    db = dot(mt_hi, c_hi) + dot(mt_lo, c_hi) + dot(mt_hi, c_lo)
    dc = dot_0(mt_hi, b_hi) + dot_0(mt_lo, b_hi) + dot_0(mt_hi, b_lo)
    b_two = jnp.concatenate([b_hi, b_lo], axis=1)
    c_two = jnp.concatenate([c_hi, c_lo], axis=1)

    def arrived(w, q):
        return jnp.concatenate([recv2[w, r * NY + q] for r in range(NZ)], axis=0)

    def scatter(w, terms, k):
        part_v[w] = terms.astype(bf16)
        for d in (4, 3, 5, 2, 6, 1, 7):
            to = lax.rem(mp + d, NMP)
            to_mp(part_v.at[w, share_of(to)], rbuf.at[w, mp], to, k)
        copy = pltpu.make_async_copy(part_v.at[w, share_of(mp)], rbuf.at[w, mp], own_sem.at[5 + w])
        copy.start()
        return copy

    def share_of(k):
        return pl.ds(pl.multiple_of(k * SHARE, SHARE), SHARE)

    def spread_share(w, out, own_part, k):
        own_part.wait()
        settle(rbuf.at[w, pl.ds(0, NMP - 1)], recv_sem.at[k])
        share = rbuf[w, 0].astype(f32)
        for d in range(1, NMP):
            share = share + rbuf[w, d].astype(f32)
        out[share_of(mp), :] = share.astype(bf16)
        for d in (4, 3, 5, 2, 6, 1, 7):
            to_mp(out.at[share_of(mp), :], out.at[share_of(mp), :], lax.rem(mp + d, NMP), k + 1)

    own_s.wait()
    settle(recv2.at[0, pl.ds(0, NB - 1)], recv_sem.at[3])
    s_in = [arrived(0, q) for q in range(NY)]
    for q in range(NY):
        dc = dc + dot_t(esdy_v[:, QW * q : QW * (q + 1)], s_in[q])
    own_dc = scatter(0, dc, 5)
    acc = colq_v[...]
    sel_r = lax.broadcasted_iota(jnp.int32, (QW, TILE), 0) // WID
    sel_l = lax.broadcasted_iota(jnp.int32, (QW, TILE), 1)

    def picks(q, base):
        return jnp.where(sel_l == sel_r + (q * (NH // NY) + base), 1.0, 0.0).astype(bf16)

    for q in range(NY):
        chi = dot(c_two, jnp.concatenate([s_in[q], s_in[q]], axis=0))
        head = chi * esdy_v[:, QW * q : QW * (q + 1)].astype(f32)
        acc = acc + dot(head.astype(bf16), picks(q, 0))
    spread_share(0, dc_out, own_dc, 5)

    own_g.wait()
    settle(recv2.at[1, pl.ds(0, NB - 1)], recv_sem.at[4])
    g_out = [arrived(1, q) for q in range(NY)]
    for q in range(NY):
        db = db + dot_t(eex_v[:, QW * q : QW * (q + 1)], g_out[q])
    own_db = scatter(1, db, 7)

    gs = jnp.zeros((8, NST), f32)
    for q in range(NY):
        span = slice(QW * q, QW * (q + 1))
        bgo = dot(b_two, jnp.concatenate([g_out[q], g_out[q]], axis=0))
        dx_v[:, span] = dx_v[:, span] + eexp_v[:, span] * bgo
        eex = eex_v[:, span].astype(f32)
        acc = acc + dot((bgo * eex).astype(bf16), picks(q, NH))
        both = jnp.sum(g_out[q].astype(f32) * s_in[q].astype(f32), axis=0, keepdims=True)
        both_hi, both_lo = halves_of(jnp.broadcast_to(both, (8, QW)))
        gs = gs + dot(both_hi, picks(q, 0)) + dot(both_lo, picks(q, 0))
    flat = acc.T
    gs_col = gs.T[0:NH, 0:1]
    head = flat[0:NH]
    tail = flat[NH : 2 * NH]
    colq = flat[2 * NH : 3 * NH]
    since = jnp.where(ti >= tj, 1.0, 0.0).astype(bf16)
    before = jnp.where(ti < tj, 1.0, 0.0).astype(bf16)
    dec = jnp.exp2(last_v[:, 0:1])
    rowq = jnp.concatenate([rowq_v[h] for h in range(NH)], axis=0)
    total = running(rowq - colq + head, since, True) + running(tail, before, False) + dec * gs_col
    dl_ref[...] = jnp.where(live, total, 0.0)

    spread_share(1, db_out, own_db, 7)

    settle(send1.at[0, pl.ds(0, NB - 1)], send_sem.at[0])
    settle(send1.at[1, pl.ds(0, NB - 1)], send_sem.at[1])
    settle(decr.at[pl.ds(0, NB - 1)], send_sem.at[2])
    settle(send2.at[0, pl.ds(0, NB - 1)], send_sem.at[3])
    settle(send2.at[1, pl.ds(0, NB - 1)], send_sem.at[4])
    for w in range(2):
        settle(rbuf.at[w, pl.ds(0, NMP - 1)], send_sem.at[5 + 2 * w])
        settle(rbuf.at[w, pl.ds(0, NMP - 1)], send_sem.at[6 + 2 * w])
    settle(rbuf.at[0, pl.ds(0, NMP - 1)], recv_sem.at[6])
    settle(rbuf.at[1, pl.ds(0, NMP - 1)], recv_sem.at[8])


def finish(xg_ref, db_ref, dc_ref, dl_ref, xg_out, db_out, dc_out, dl_out, db_v, dc_v, sem):
    copies = [pltpu.make_async_copy(xg_ref, xg_out, sem.at[0]), pltpu.make_async_copy(dl_ref, dl_out, sem.at[1])]
    for copy in copies:
        copy.start()
    for k, (low, wide, out) in enumerate(((db_ref, db_v, db_out), (dc_ref, dc_v, dc_out))):
        wide[...] = low[...].astype(f32)
        copy = pltpu.make_async_copy(wide, out, sem.at[2 + k])
        copy.start()
        copies.append(copy)
    for copy in copies:
        copy.wait()


def on_device(x_in, dy_out, b_in, c_in, log_decay, parents, lengths):
    vmem = pl.BlockSpec(memory_space=pltpu.VMEM)
    smem = pl.BlockSpec(memory_space=pltpu.SMEM)
    anywhere = pl.BlockSpec(memory_space=pl.ANY)
    wide = (ROWS, CH)
    dma = pltpu.SemaphoreType.DMA
    given = pl.pallas_call(
        kernel,
        out_shape=(
            pltpu.VMEM(wide, f32),
            pltpu.VMEM((ROWS, NST), bf16),
            pltpu.VMEM((ROWS, NST), bf16),
            pltpu.VMEM((NH, ROWS), f32),
        ),
        in_specs=[smem, vmem, anywhere, anywhere, vmem, vmem, vmem],
        out_specs=(vmem, vmem, vmem, vmem),
        scratch_shapes=[
            pltpu.VMEM(wide, f32),
            pltpu.VMEM(wide, f32),
            pltpu.VMEM(wide, bf16),
            pltpu.VMEM(wide, bf16),
            pltpu.VMEM(wide, f32),
            pltpu.VMEM((2, NST, ROWS), bf16),
            pltpu.VMEM((2, NST, ROWS), bf16),
            pltpu.VMEM((NH, ROWS, TILE), f32),
            pltpu.VMEM((NH, 1, ROWS), f32),
            pltpu.VMEM((NH, TILE), f32),
            pltpu.VMEM((ROWS, ROWS), f32),
            pltpu.VMEM((ROWS, ROWS), f32),
            pltpu.VMEM((NH, 1, ROWS), f32),
            pltpu.VMEM((ROWS, TILE), f32),
            pltpu.VMEM((NB, TILE), jnp.int32),
            pltpu.SMEM((NB, TILE), jnp.int32),
            pltpu.VMEM((2, NB, RW, QW), bf16),
            pltpu.VMEM((2, NB, RW, QW), bf16),
            pltpu.VMEM((NY, 1, QW), f32),
            pltpu.VMEM((NB, 1, QW), f32),
            pltpu.VMEM((NB + 1, RW, QW), f32),
            pltpu.VMEM((NB + 1, RW, QW), f32),
            pltpu.VMEM((2, NB, RW, QW), bf16),
            pltpu.VMEM((2, NB, RW, QW), bf16),
            pltpu.VMEM((2, ROWS, NST), bf16),
            pltpu.VMEM((2, NMP, SHARE, NST), bf16),
            dma((2 * NY,)),
            dma,
            dma((9,)),
            dma((9,)),
            dma((7,)),
        ],
        compiler_params=pltpu.CompilerParams(
            collective_id=0, has_side_effects=True, vmem_limit_bytes=52 * 1024 * 1024
        ),
    )(lengths, parents.reshape(1, NB), x_in, dy_out, b_in, c_in, log_decay)
    return tuple(
        pl.pallas_call(
            finish,
            out_shape=(
                jax.ShapeDtypeStruct(wide, f32),
                jax.ShapeDtypeStruct((ROWS, NST), f32),
                jax.ShapeDtypeStruct((ROWS, NST), f32),
                jax.ShapeDtypeStruct((NH, ROWS), f32),
            ),
            in_specs=[vmem] * 4,
            out_specs=(anywhere,) * 4,
            scratch_shapes=[
                pltpu.VMEM((ROWS, NST), f32),
                pltpu.VMEM((ROWS, NST), f32),
                dma((4,)),
            ],
        )(*(pltpu.with_memory_space_constraint(g, pltpu.VMEM) for g in given))
    )


def solution(mesh):
    return jax.shard_map(
        on_device,
        mesh=mesh,
        in_specs=(
            P("seq", "mp"),
            P("seq", "mp"),
            P("seq", None),
            P("seq", None),
            P("mp", "seq"),
            P(),
            P(),
        ),
        out_specs=(P("seq", "mp"), P("seq", None), P("seq", None), P("mp", "seq")),
        check_vma=False,
    )
```

```python
import functools
import math

import jax
import jax.numpy as jnp
from jax import lax
from jax.experimental import pallas as pl
from jax.experimental.pallas import tpu as pltpu
from jax.sharding import PartitionSpec as P

f32 = jnp.float32
bf16 = jnp.bfloat16
MESH = pl.DeviceIdType.MESH
LOG2E = math.log2(math.e)

ROWS = 512
NST = 128
NH = 16
WID = 64
CH = NH * WID
TILE = 128
NT = ROWS // TILE
NY = 4
NZ = 8
NB = NY * NZ
QW = CH // NY
RW = NST // NZ
NMP = 8
SHARE = ROWS // NMP
CUT1, CUT2 = 3, 6
DZ_ORDER = (4, 3, 5, 2, 6, 1, 7, 0)


def dot(a, b):
    return jnp.dot(a, b, preferred_element_type=f32)


def dot_t(a, b):
    return lax.dot_general(a, b, (((1,), (1,)), ((), ())), preferred_element_type=f32)


def dot_0(a, b):
    return lax.dot_general(a, b, (((0,), (0,)), ((), ())), preferred_element_type=f32)


def split3(v):
    hi = v.astype(bf16)
    rest = v - hi.astype(f32)
    mid = rest.astype(bf16)
    low = (rest - mid.astype(f32)).astype(bf16)
    return hi, mid, low


def running(v, tri, reverse):
    tall = jnp.concatenate([v[:, TILE * i : TILE * (i + 1)] for i in range(NT)], axis=0)
    hi, mid, low = split3(tall)
    part = dot(hi, tri) + dot(mid, tri) + dot(low, tri)
    whole = jnp.sum(tall, axis=1, keepdims=True)
    pieces = [None] * NT
    carry = jnp.zeros((NH, 1), f32)
    order = range(NT - 1, -1, -1) if reverse else range(NT)
    for i in order:
        rows = slice(NH * i, NH * (i + 1))
        pieces[i] = part[rows] + carry
        carry = carry + whole[rows]
    return jnp.concatenate(pieces, axis=1)


def halves_of(v):
    hi = v.astype(bf16)
    return hi, (v - hi.astype(f32)).astype(bf16)


def kernel(
    lengths_hbm,
    prow_hbm,
    x_hbm,
    dy_hbm,
    b_hbm,
    c_hbm,
    logd_hbm,
    dx_v,
    db_out,
    dc_out,
    dl_ref,
    lengths,
    prow,
    b_ref,
    c_ref,
    logd_ref,
    x_v,
    dy_v,
    eex_v,
    esdy_v,
    eexp_v,
    bt_v,
    ct_v,
    ccol_v,
    crow_v,
    last_v,
    st_v,
    mt_v,
    rowq_v,
    colq_v,
    tab_v,
    tab_s,
    send1,
    recv1,
    decx,
    decr,
    decw,
    f_v,
    r_v,
    send2,
    recv2,
    part_v,
    rbuf,
    load_sem,
    tab_sem,
    send_sem,
    recv_sem,
    own_sem,
):
    me = lax.axis_index("seq")
    mp = lax.axis_index("mp")
    my_y = lax.rem(me, NY)
    my_z = me // NY

    def group(i):
        return lax.rem(my_y + i, NY)

    def peer(i, dz):
        return lax.rem(my_z + dz, NZ) * NY + group(i)

    def lanes(q):
        return pl.ds(pl.multiple_of(q * QW, QW), QW)

    def to_seq(src, dst, j, k):
        pltpu.make_async_remote_copy(
            src_ref=src,
            dst_ref=dst,
            send_sem=send_sem.at[k],
            recv_sem=recv_sem.at[k],
            device_id={"seq": j},
            device_id_type=MESH,
        ).start()

    def to_mp(src, dst, j, k):
        pltpu.make_async_remote_copy(
            src_ref=src,
            dst_ref=dst,
            send_sem=send_sem.at[k],
            recv_sem=recv_sem.at[k],
            device_id={"mp": j},
            device_id_type=MESH,
        ).start()

    def settle(like, sem):
        pltpu.make_async_copy(like, like, sem).wait()

    loads = []

    def load(src, dst):
        copy = pltpu.make_async_copy(src, dst, load_sem.at[len(loads)])
        copy.start()
        loads.append(copy)
        return copy

    logd_in = load(logd_hbm, logd_ref)
    lengths_in = load(lengths_hbm, lengths)
    b_in = load(b_hbm, b_ref)
    x_in = [load(x_hbm.at[:, lanes(group(i))], x_v.at[:, lanes(group(i))]) for i in range(NY)]

    barrier = pltpu.get_barrier_semaphore()
    for i in range(NY):
        for dz in DZ_ORDER:
            if i or dz:
                pl.semaphore_signal(barrier, inc=1, device_id={"seq": peer(i, dz)}, device_id_type=MESH)
    for k in range(1, NMP):
        pl.semaphore_signal(barrier, inc=1, device_id={"mp": lax.rem(mp + k, NMP)}, device_id_type=MESH)

    c_in = load(c_hbm, c_ref)
    dy_in = [load(dy_hbm.at[:, lanes(group(i))], dy_v.at[:, lanes(group(i))]) for i in range(NY)]
    prow_in = load(prow_hbm, prow)

    lengths_in.wait()
    length = lengths[0, me]
    logd_in.wait()

    ti = lax.broadcasted_iota(jnp.int32, (TILE, TILE), 0)
    tj = lax.broadcasted_iota(jnp.int32, (TILE, TILE), 1)
    upto = jnp.where(ti <= tj, 1.0, 0.0).astype(bf16)
    lane = lax.broadcasted_iota(jnp.int32, (NH, ROWS), 1)
    live = lane < length
    logd = jnp.where(live, logd_ref[...] * LOG2E, 0.0)
    cum = running(logd, upto, False)
    last = cum[:, ROWS - 1 : ROWS]
    last_v[...] = jnp.broadcast_to(last, (NH, TILE))
    ee = jnp.where(live, jnp.exp2(last - cum), 0.0)
    es = jnp.exp2(cum)
    ee_hi = ee.astype(bf16).astype(f32)
    es_hi = es.astype(bf16).astype(f32)
    stack = jnp.concatenate(
        [ee_hi, ee - ee_hi, es_hi, es - es_hi, cum, jnp.zeros((NST - 5 * NH, ROWS), f32)], axis=0
    )
    cols = stack.T
    decx[0] = cols[ROWS - 1 :, :]
    cols_b = cols.astype(bf16)
    b_in.wait()
    bt_hi, bt_lo = halves_of(b_ref[...].T)
    bt_v[0] = bt_hi
    bt_v[1] = bt_lo

    er = lax.broadcasted_iota(jnp.int32, (NST, QW), 0)
    eh = lax.broadcasted_iota(jnp.int32, (NST, QW), 1) // WID

    def spread(q, base):
        head = eh + (q * (NH // NY) + base)
        return dot(cols_b, jnp.where((er == head) | (er == head + NH), 1.0, 0.0).astype(bf16))

    def state_of(t_v, wide):
        hi, low = halves_of(wide)
        total = dot(t_v[0], hi) + dot(t_v[1], hi) + dot(t_v[0], low)
        return hi, total.astype(bf16)

    for i in range(NY):
        q = group(i)
        e_wide = spread(q, 0)
        eexp_v[:, lanes(q)] = e_wide
        x_in[i].wait()
        hi, loc = state_of(bt_v, x_v[:, lanes(q)] * e_wide)
        eex_v[:, lanes(q)] = hi
        for r in range(NZ):
            send1[0, r * NY + q] = loc[RW * r : RW * (r + 1), :]
        if i == 0:
            pl.semaphore_wait(barrier, NB - 1 + NMP - 1)
        for dz in DZ_ORDER:
            if i or dz:
                j = peer(i, dz)
                to_seq(decx.at[0], decr.at[me], j, 2)
                to_seq(send1.at[0, j], recv1.at[0, me], j, 0)

    c_in.wait()
    ct_hi, ct_lo = halves_of(c_ref[...].T)
    ct_v[0] = ct_hi
    ct_v[1] = ct_lo
    row_live = lax.broadcasted_iota(jnp.int32, (ROWS, QW), 0) < length
    for i in range(NY):
        q = group(i)
        s_wide = spread(q, 2 * NH)
        dy_in[i].wait()
        dy = jnp.where(row_live, dy_v[:, lanes(q)], 0.0)
        dy_v[:, lanes(q)] = dy
        hi, loc = state_of(ct_v, dy * s_wide)
        esdy_v[:, lanes(q)] = hi
        for r in range(NZ):
            send1[1, r * NY + q] = loc[RW * r : RW * (r + 1), :]
        for dz in DZ_ORDER:
            if i or dz:
                j = peer(i, dz)
                to_seq(send1.at[1, j], recv1.at[1, me], j, 1)
    own = [
        pltpu.make_async_copy(send1.at[0, me], recv1.at[0, me], own_sem.at[0]),
        pltpu.make_async_copy(send1.at[1, me], recv1.at[1, me], own_sem.at[1]),
        pltpu.make_async_copy(decx.at[0], decr.at[me], own_sem.at[2]),
    ]
    for copy in own:
        copy.start()

    prow_in.wait()
    bi = lax.broadcasted_iota(jnp.int32, (NB, NB), 0)
    bj = lax.broadcasted_iota(jnp.int32, (NB, NB), 1)
    par = jnp.broadcast_to(prow[...], (NB, NB))
    par_col = jnp.sum(jnp.where(bi == bj, par, 0), axis=1, keepdims=True)
    first = jnp.min(jnp.where(par == bi, bj, NB), axis=1, keepdims=True)
    sibling = jnp.min(jnp.where((par == par_col) & (bj > bi), bj, NB), axis=1, keepdims=True)
    tl = lax.broadcasted_iota(jnp.int32, (NB, TILE), 1)
    tab_v[...] = jnp.where(
        tl == 0, first, jnp.where(tl == 1, sibling, jnp.where(par_col < 0, NB, par_col))
    )
    tab = pltpu.make_async_copy(tab_v, tab_s, tab_sem)
    tab.start()

    st_v[...] = lax.dot_general(
        b_ref[...],
        c_ref[...],
        (((1,), (1,)), ((), ())),
        preferred_element_type=f32,
        precision=lax.Precision.HIGHEST,
    )
    mt_v[...] = jnp.zeros_like(mt_v)
    colq_v[...] = jnp.zeros_like(colq_v)
    for h in range(NH):
        crow_v[h] = cum[h : h + 1, :]
        ccol_v[h] = jnp.broadcast_to(cols[:, 4 * NH + h : 4 * NH + h + 1], (ROWS, TILE))
    left = lax.broadcasted_iota(jnp.int32, (ROWS, TILE), 1) < WID
    nil = jnp.zeros((ROWS, TILE), bf16)

    def pair(k, carry):
        span = pl.ds(pl.multiple_of(k * TILE, TILE), TILE)
        xk = x_v[:, span]
        dk = dy_v[:, span]
        xr = pltpu.roll(xk, WID, 1)
        dr = pltpu.roll(dk, WID, 1)
        xs, ds = [], []
        for s in range(2):
            hi, low = halves_of(jnp.where(left, xk, xr) if s == 0 else jnp.where(left, xr, xk))
            both = jnp.where(left, hi, low)
            xs.append(jnp.concatenate([both, both], axis=1))
            ds.append(halves_of(jnp.where(left, dk, dr) if s == 0 else jnp.where(left, dr, dk)))
        dg = [jnp.concatenate(d, axis=1) for d in ds]
        dn = [jnp.where(left, ds[0][0], nil), jnp.where(left, nil, ds[1][0])]
        dx = [jnp.zeros((TILE, TILE), f32) for _ in range(NT)]
        rowq = [[None] * NT, [None] * NT]
        colq = [[None] * NT, [None] * NT]
        for ib in range(NT):
            ts = slice(TILE * ib, TILE * (ib + 1))
            dt = jnp.concatenate([dn[0][ts, :], dn[1][ts, :]], axis=0)
            for jb in range(ib + 1):
                us = slice(TILE * jb, TILE * (jb + 1))
                score = st_v[us, ts]
                total = mt_v[us, ts]
                wide = []
                for s in range(2):
                    h = 2 * k + s
                    g = dot_t(xs[s][us, :], dg[s][ts, :])
                    diff = crow_v[h, :, ts] - ccol_v[h, us, :]
                    if ib == jb:
                        diff = jnp.where(tj >= ti, diff, -1e30)
                    e = jnp.exp2(diff)
                    dsc = e * score
                    total = total + e * g
                    wide.append(dsc.astype(bf16))
                    joint = dsc * g
                    down = jnp.sum(joint, axis=0, keepdims=True)
                    rowq[s][ib] = down if jb == 0 else rowq[s][ib] + down
                    colq[s][jb] = joint if ib == jb else colq[s][jb] + joint
                mt_v[us, ts] = total
                dx[jb] = dx[jb] + dot(jnp.concatenate(wide, axis=1), dt)
        for s in range(2):
            rowq_v[2 * k + s] = jnp.concatenate(rowq[s], axis=1)
        for jb in range(NT):
            us = slice(TILE * jb, TILE * (jb + 1))
            both = colq_v[us, :]
            for s in range(2):
                tot = jnp.sum(colq[s][jb], axis=1, keepdims=True)
                both = jnp.where(tj == 2 * NH + 2 * k + s, tot, both)
            colq_v[us, :] = both
            dx_v[us, span] = dx[jb]
        return carry

    lax.fori_loop(0, CUT1, pair, 0)

    tab.wait()
    for copy in own:
        copy.wait()
    f_v[NB] = jnp.zeros((RW, QW), f32)
    r_v[NB] = jnp.zeros((RW, QW), f32)
    settle(recv1.at[0, pl.ds(0, NB - 1)], recv_sem.at[0])
    settle(decr.at[pl.ds(0, NB - 1)], recv_sem.at[2])
    mine = eh + (my_y * (NH // NY) + 2 * NH)
    widen = jnp.where((er == mine) | (er == mine + NH), 1.0, 0.0).astype(bf16)
    dec_rows = jnp.concatenate([decr[b] for b in range(NB)], axis=0).astype(bf16)
    dec_wide = dot(dec_rows, widen)
    for b in range(NB):
        decw[b] = dec_wide[b : b + 1, :]

    def forward(b, carry):
        state = f_v[tab_s[b, 2]]
        send2[0, b] = state.astype(bf16)
        f_v[b] = recv1[0, b].astype(f32) + decw[b] * state
        return carry

    def backward(k, carry):
        a = NB - 1 - k
        adj = r_v[tab_s[a, 0]]
        send2[1, a] = adj.astype(bf16)
        r_v[a] = recv1[1, a].astype(f32) + decw[a] * adj + r_v[tab_s[a, 1]]
        return carry

    def hand_back(w, k):
        for i in range(NY):
            for dz in DZ_ORDER:
                if i or dz:
                    j = peer(i, dz)
                    to_seq(send2.at[w, j], recv2.at[w, me], j, k + i)
        copy = pltpu.make_async_copy(send2.at[w, me], recv2.at[w, me], own_sem.at[3 + w])
        copy.start()
        return copy

    lax.fori_loop(0, NB, forward, 0)
    own_s = hand_back(0, 9)

    lax.fori_loop(CUT1, CUT2, pair, 0)

    settle(recv1.at[1, pl.ds(0, NB - 1)], recv_sem.at[1])
    lax.fori_loop(0, NB, backward, 0)
    own_g = hand_back(1, 9 + NY)

    lax.fori_loop(CUT2, NH // 2, pair, 0)

    b_hi, b_lo = halves_of(b_ref[...])
    c_hi, c_lo = halves_of(c_ref[...])
    mt_hi, mt_lo = halves_of(mt_v[...])
    db = dot(mt_hi, c_hi) + dot(mt_lo, c_hi) + dot(mt_hi, c_lo)
    dc = dot_0(mt_hi, b_hi) + dot_0(mt_lo, b_hi) + dot_0(mt_hi, b_lo)
    b_two = jnp.concatenate([b_hi, b_lo], axis=1)
    c_two = jnp.concatenate([c_hi, c_lo], axis=1)

    def arrived(w, i, own_part):
        count = NZ if i else NZ - 1
        if i == 0:
            own_part.wait()
        settle(recv2.at[w, pl.ds(0, count)], recv_sem.at[9 + NY * w + i])
        return jnp.concatenate([recv2[w, r * NY + source(i)] for r in range(NZ)], axis=0)

    def source(i):
        return lax.rem(my_y + (NY - i), NY)

    def scatter(w, terms, k):
        part_v[w] = terms.astype(bf16)
        for d in (4, 3, 5, 2, 6, 1, 7):
            to = lax.rem(mp + d, NMP)
            to_mp(part_v.at[w, share_of(to)], rbuf.at[w, mp], to, k)
        copy = pltpu.make_async_copy(part_v.at[w, share_of(mp)], rbuf.at[w, mp], own_sem.at[5 + w])
        copy.start()
        return copy

    def share_of(k):
        return pl.ds(pl.multiple_of(k * SHARE, SHARE), SHARE)

    def spread_share(w, out, own_part, k):
        own_part.wait()
        settle(rbuf.at[w, pl.ds(0, NMP - 1)], recv_sem.at[k])
        share = rbuf[w, 0].astype(f32)
        for d in range(1, NMP):
            share = share + rbuf[w, d].astype(f32)
        out[share_of(mp), :] = share.astype(bf16)
        for d in (4, 3, 5, 2, 6, 1, 7):
            to_mp(out.at[share_of(mp), :], out.at[share_of(mp), :], lax.rem(mp + d, NMP), k + 1)

    s_in = []
    for i in range(NY):
        s_in.append(arrived(0, i, own_s))
        dc = dc + dot_t(esdy_v[:, lanes(source(i))], s_in[i])
    own_dc = scatter(0, dc, 5)
    acc = colq_v[...]
    sel_r = lax.broadcasted_iota(jnp.int32, (QW, TILE), 0) // WID
    sel_l = lax.broadcasted_iota(jnp.int32, (QW, TILE), 1)

    def picks(q, base):
        return jnp.where(sel_l == sel_r + (q * (NH // NY) + base), 1.0, 0.0).astype(bf16)

    for i in range(NY):
        chi = dot(c_two, jnp.concatenate([s_in[i], s_in[i]], axis=0))
        head = chi * esdy_v[:, lanes(source(i))].astype(f32)
        acc = acc + dot(head.astype(bf16), picks(source(i), 0))
    spread_share(0, dc_out, own_dc, 5)

    g_out = []
    for i in range(NY):
        g_out.append(arrived(1, i, own_g))
        db = db + dot_t(eex_v[:, lanes(source(i))], g_out[i])
    own_db = scatter(1, db, 7)

    gs = jnp.zeros((8, NST), f32)
    for i in range(NY):
        q = source(i)
        span = lanes(q)
        bgo = dot(b_two, jnp.concatenate([g_out[i], g_out[i]], axis=0))
        dx_v[:, span] = dx_v[:, span] + eexp_v[:, span] * bgo
        eex = eex_v[:, span].astype(f32)
        acc = acc + dot((bgo * eex).astype(bf16), picks(q, NH))
        both = jnp.sum(g_out[i].astype(f32) * s_in[i].astype(f32), axis=0, keepdims=True)
        both_hi, both_lo = halves_of(jnp.broadcast_to(both, (8, QW)))
        gs = gs + dot(both_hi, picks(q, 0)) + dot(both_lo, picks(q, 0))
    flat = acc.T
    gs_col = gs.T[0:NH, 0:1]
    head = flat[0:NH]
    tail = flat[NH : 2 * NH]
    colq = flat[2 * NH : 3 * NH]
    since = jnp.where(ti >= tj, 1.0, 0.0).astype(bf16)
    before = jnp.where(ti < tj, 1.0, 0.0).astype(bf16)
    dec = jnp.exp2(last_v[:, 0:1])
    rowq = jnp.concatenate([rowq_v[h] for h in range(NH)], axis=0)
    total = running(rowq - colq + head, since, True) + running(tail, before, False) + dec * gs_col
    dl_ref[...] = jnp.where(live, total, 0.0)

    spread_share(1, db_out, own_db, 7)

    settle(send1.at[0, pl.ds(0, NB - 1)], send_sem.at[0])
    settle(send1.at[1, pl.ds(0, NB - 1)], send_sem.at[1])
    settle(decr.at[pl.ds(0, NB - 1)], send_sem.at[2])
    for k in range(2 * NY):
        settle(send2.at[0, pl.ds(0, NZ if k % NY else NZ - 1)], send_sem.at[9 + k])
    for w in range(2):
        settle(rbuf.at[w, pl.ds(0, NMP - 1)], send_sem.at[5 + 2 * w])
        settle(rbuf.at[w, pl.ds(0, NMP - 1)], send_sem.at[6 + 2 * w])
    settle(rbuf.at[0, pl.ds(0, NMP - 1)], recv_sem.at[6])
    settle(rbuf.at[1, pl.ds(0, NMP - 1)], recv_sem.at[8])


def finish(xg_ref, db_ref, dc_ref, dl_ref, xg_out, db_out, dc_out, dl_out, db_v, dc_v, sem):
    copies = [pltpu.make_async_copy(xg_ref, xg_out, sem.at[0]), pltpu.make_async_copy(dl_ref, dl_out, sem.at[1])]
    for copy in copies:
        copy.start()
    for k, (low, wide, out) in enumerate(((db_ref, db_v, db_out), (dc_ref, dc_v, dc_out))):
        wide[...] = low[...].astype(f32)
        copy = pltpu.make_async_copy(wide, out, sem.at[2 + k])
        copy.start()
        copies.append(copy)
    for copy in copies:
        copy.wait()


def on_device(x_in, dy_out, b_in, c_in, log_decay, parents, lengths):
    vmem = pl.BlockSpec(memory_space=pltpu.VMEM)
    anywhere = pl.BlockSpec(memory_space=pl.ANY)
    wide = (ROWS, CH)
    dma = pltpu.SemaphoreType.DMA
    given = pl.pallas_call(
        kernel,
        out_shape=(
            pltpu.VMEM(wide, f32),
            pltpu.VMEM((ROWS, NST), bf16),
            pltpu.VMEM((ROWS, NST), bf16),
            pltpu.VMEM((NH, ROWS), f32),
        ),
        in_specs=[anywhere] * 7,
        out_specs=(vmem, vmem, vmem, vmem),
        scratch_shapes=[
            pltpu.SMEM((1, NB), jnp.int32),
            pltpu.VMEM((1, NB), jnp.int32),
            pltpu.VMEM((ROWS, NST), f32),
            pltpu.VMEM((ROWS, NST), f32),
            pltpu.VMEM((NH, ROWS), f32),
            pltpu.VMEM(wide, f32),
            pltpu.VMEM(wide, f32),
            pltpu.VMEM(wide, bf16),
            pltpu.VMEM(wide, bf16),
            pltpu.VMEM(wide, f32),
            pltpu.VMEM((2, NST, ROWS), bf16),
            pltpu.VMEM((2, NST, ROWS), bf16),
            pltpu.VMEM((NH, ROWS, TILE), f32),
            pltpu.VMEM((NH, 1, ROWS), f32),
            pltpu.VMEM((NH, TILE), f32),
            pltpu.VMEM((ROWS, ROWS), f32),
            pltpu.VMEM((ROWS, ROWS), f32),
            pltpu.VMEM((NH, 1, ROWS), f32),
            pltpu.VMEM((ROWS, TILE), f32),
            pltpu.VMEM((NB, TILE), jnp.int32),
            pltpu.SMEM((NB, TILE), jnp.int32),
            pltpu.VMEM((2, NB, RW, QW), bf16),
            pltpu.VMEM((2, NB, RW, QW), bf16),
            pltpu.VMEM((1, 1, NST), f32),
            pltpu.VMEM((NB, 1, NST), f32),
            pltpu.VMEM((NB, 1, QW), f32),
            pltpu.VMEM((NB + 1, RW, QW), f32),
            pltpu.VMEM((NB + 1, RW, QW), f32),
            pltpu.VMEM((2, NB, RW, QW), bf16),
            pltpu.VMEM((2, NB, RW, QW), bf16),
            pltpu.VMEM((2, ROWS, NST), bf16),
            pltpu.VMEM((2, NMP, SHARE, NST), bf16),
            dma((2 * NY + 5,)),
            dma,
            dma((9 + 2 * NY,)),
            dma((9 + 2 * NY,)),
            dma((7,)),
        ],
        compiler_params=pltpu.CompilerParams(
            collective_id=0, has_side_effects=True, vmem_limit_bytes=52 * 1024 * 1024
        ),
    )(lengths.reshape(1, NB), parents.reshape(1, NB), x_in, dy_out, b_in, c_in, log_decay)
    return tuple(
        pl.pallas_call(
            finish,
            out_shape=(
                jax.ShapeDtypeStruct(wide, f32),
                jax.ShapeDtypeStruct((ROWS, NST), f32),
                jax.ShapeDtypeStruct((ROWS, NST), f32),
                jax.ShapeDtypeStruct((NH, ROWS), f32),
            ),
            in_specs=[vmem] * 4,
            out_specs=(anywhere,) * 4,
            scratch_shapes=[
                pltpu.VMEM((ROWS, NST), f32),
                pltpu.VMEM((ROWS, NST), f32),
                dma((4,)),
            ],
        )(*(pltpu.with_memory_space_constraint(g, pltpu.VMEM) for g in given))
    )


def solution(mesh):
    return jax.shard_map(
        on_device,
        mesh=mesh,
        in_specs=(
            P("seq", "mp"),
            P("seq", "mp"),
            P("seq", None),
            P("seq", None),
            P("mp", "seq"),
            P(),
            P(),
        ),
        out_specs=(P("seq", "mp"), P("seq", None), P("seq", None), P("mp", "seq")),
        check_vma=False,
    )
```

```python
import functools
import math

import jax
import jax.numpy as jnp
from jax import lax
from jax.experimental import pallas as pl
from jax.experimental.pallas import tpu as pltpu
from jax.sharding import PartitionSpec as P

f32 = jnp.float32
bf16 = jnp.bfloat16
MESH = pl.DeviceIdType.MESH
LOG2E = math.log2(math.e)

ROWS = 512
NST = 128
NH = 16
WID = 64
CH = NH * WID
TILE = 128
NT = ROWS // TILE
NY = 4
NZ = 8
NB = NY * NZ
QW = CH // NY
RW = NST // NZ
NMP = 8
SHARE = ROWS // NMP
CUT = 3
DZ_ORDER = (4, 3, 5, 2, 6, 1, 7, 0)


def dot(a, b):
    return jnp.dot(a, b, preferred_element_type=f32)


def dot_t(a, b):
    return lax.dot_general(a, b, (((1,), (1,)), ((), ())), preferred_element_type=f32)


def dot_0(a, b):
    return lax.dot_general(a, b, (((0,), (0,)), ((), ())), preferred_element_type=f32)


def split3(v):
    hi = v.astype(bf16)
    rest = v - hi.astype(f32)
    mid = rest.astype(bf16)
    low = (rest - mid.astype(f32)).astype(bf16)
    return hi, mid, low


def running(v, tri, reverse):
    tall = jnp.concatenate([v[:, TILE * i : TILE * (i + 1)] for i in range(NT)], axis=0)
    hi, mid, low = split3(tall)
    part = dot(hi, tri) + dot(mid, tri) + dot(low, tri)
    whole = jnp.sum(tall, axis=1, keepdims=True)
    pieces = [None] * NT
    carry = jnp.zeros((NH, 1), f32)
    order = range(NT - 1, -1, -1) if reverse else range(NT)
    for i in order:
        rows = slice(NH * i, NH * (i + 1))
        pieces[i] = part[rows] + carry
        carry = carry + whole[rows]
    return jnp.concatenate(pieces, axis=1)


def halves_of(v):
    hi = v.astype(bf16)
    return hi, (v - hi.astype(f32)).astype(bf16)


def kernel(
    lengths_hbm,
    prow_hbm,
    x_hbm,
    dy_hbm,
    b_hbm,
    c_hbm,
    logd_hbm,
    dx_v,
    db_out,
    dc_out,
    dl_ref,
    lengths,
    prow,
    b_ref,
    c_ref,
    logd_ref,
    x_v,
    dy_v,
    eex_v,
    esdy_v,
    eexp_v,
    bt_v,
    ct_v,
    ccol_v,
    crow_v,
    last_v,
    st_v,
    mt_v,
    rowq_v,
    colq_v,
    tab_v,
    tab_s,
    send1,
    recv1,
    decx,
    decr,
    decw,
    f_v,
    r_v,
    send2,
    recv2,
    sum_v,
    part_v,
    rbuf,
    load_sem,
    tab_sem,
    send_sem,
    recv_sem,
    own_sem,
):
    me = lax.axis_index("seq")
    mp = lax.axis_index("mp")
    my_y = lax.rem(me, NY)
    my_z = me // NY

    def group(i):
        return lax.rem(my_y + i, NY)

    def peer(i, dz):
        return lax.rem(my_z + dz, NZ) * NY + group(i)

    def lanes(q):
        return pl.ds(pl.multiple_of(q * QW, QW), QW)

    def to_seq(src, dst, j, k):
        pltpu.make_async_remote_copy(
            src_ref=src,
            dst_ref=dst,
            send_sem=send_sem.at[k],
            recv_sem=recv_sem.at[k],
            device_id={"seq": j},
            device_id_type=MESH,
        ).start()

    def to_mp(src, dst, j, k):
        pltpu.make_async_remote_copy(
            src_ref=src,
            dst_ref=dst,
            send_sem=send_sem.at[k],
            recv_sem=recv_sem.at[k],
            device_id={"mp": j},
            device_id_type=MESH,
        ).start()

    def settle(like, sem):
        pltpu.make_async_copy(like, like, sem).wait()

    barrier = pltpu.get_barrier_semaphore()
    for i in range(NY):
        for dz in DZ_ORDER:
            if i or dz:
                pl.semaphore_signal(barrier, inc=1, device_id={"seq": peer(i, dz)}, device_id_type=MESH)
    for k in range(1, NMP):
        pl.semaphore_signal(barrier, inc=1, device_id={"mp": lax.rem(mp + k, NMP)}, device_id_type=MESH)

    loads = []

    def load(src, dst):
        copy = pltpu.make_async_copy(src, dst, load_sem.at[len(loads)])
        copy.start()
        loads.append(copy)
        return copy

    logd_in = load(logd_hbm, logd_ref)
    lengths_in = load(lengths_hbm, lengths)
    b_in = load(b_hbm, b_ref)
    x_in = [load(x_hbm.at[:, lanes(group(i))], x_v.at[:, lanes(group(i))]) for i in range(NY)]

    c_in = load(c_hbm, c_ref)
    dy_in = [load(dy_hbm.at[:, lanes(group(i))], dy_v.at[:, lanes(group(i))]) for i in range(NY)]
    prow_in = load(prow_hbm, prow)

    lengths_in.wait()
    length = lengths[0, me]
    logd_in.wait()

    ti = lax.broadcasted_iota(jnp.int32, (TILE, TILE), 0)
    tj = lax.broadcasted_iota(jnp.int32, (TILE, TILE), 1)
    upto = jnp.where(ti <= tj, 1.0, 0.0).astype(bf16)
    lane = lax.broadcasted_iota(jnp.int32, (NH, ROWS), 1)
    live = lane < length
    logd = jnp.where(live, logd_ref[...] * LOG2E, 0.0)
    cum = running(logd, upto, False)
    last = cum[:, ROWS - 1 : ROWS]
    last_v[...] = jnp.broadcast_to(last, (NH, TILE))
    ee = jnp.where(live, jnp.exp2(last - cum), 0.0)
    es = jnp.exp2(cum)
    ee_hi = ee.astype(bf16).astype(f32)
    es_hi = es.astype(bf16).astype(f32)
    stack = jnp.concatenate(
        [ee_hi, ee - ee_hi, es_hi, es - es_hi, cum, jnp.zeros((NST - 5 * NH, ROWS), f32)], axis=0
    )
    cols = stack.T
    decx[0] = cols[ROWS - 1 :, :]
    cols_b = cols.astype(bf16)
    b_in.wait()
    bt_hi, bt_lo = halves_of(b_ref[...].T)
    bt_v[0] = bt_hi
    bt_v[1] = bt_lo

    er = lax.broadcasted_iota(jnp.int32, (NST, QW), 0)
    eh = lax.broadcasted_iota(jnp.int32, (NST, QW), 1) // WID

    def spread(q, base):
        head = eh + (q * (NH // NY) + base)
        return dot(cols_b, jnp.where((er == head) | (er == head + NH), 1.0, 0.0).astype(bf16))

    def state_of(t_v, wide):
        hi, low = halves_of(wide)
        total = dot(t_v[0], hi) + dot(t_v[1], hi) + dot(t_v[0], low)
        return hi, low, total.astype(bf16)

    def end_group(i, carry):
        q = group(i)
        e_wide = spread(q, 0)
        eexp_v[:, lanes(q)] = e_wide
        pltpu.make_async_copy(x_hbm.at[:, lanes(q)], x_v.at[:, lanes(q)], load_sem.at[3 + i]).wait()
        hi, low, loc = state_of(bt_v, x_v[:, lanes(q)] * e_wide)
        eex_v[0, :, lanes(q)] = hi
        eex_v[1, :, lanes(q)] = low
        for r in range(NZ):
            send1[0, r * NY + q] = loc[RW * r : RW * (r + 1), :]

        @pl.when(i == 0)
        def _():
            pl.semaphore_wait(barrier, NB - 1 + NMP - 1)

        def away(dz):
            j = peer(i, dz)
            to_seq(decx.at[0], decr.at[me], j, 2)
            to_seq(send1.at[0, j], recv1.at[0, me], j, 0)

        for dz in DZ_ORDER:
            if dz:
                away(dz)
        pl.when(i > 0)(lambda: away(0))
        return carry

    lax.fori_loop(0, NY, end_group, 0)

    c_in.wait()
    ct_hi, ct_lo = halves_of(c_ref[...].T)
    ct_v[0] = ct_hi
    ct_v[1] = ct_lo
    row_live = lax.broadcasted_iota(jnp.int32, (ROWS, QW), 0) < length
    def adj_group(i, carry):
        q = group(i)
        s_wide = spread(q, 2 * NH)
        pltpu.make_async_copy(dy_hbm.at[:, lanes(q)], dy_v.at[:, lanes(q)], load_sem.at[4 + NY + i]).wait()
        dy = jnp.where(row_live, dy_v[:, lanes(q)], 0.0)
        dy_v[:, lanes(q)] = dy
        hi, low, loc = state_of(ct_v, dy * s_wide)
        esdy_v[0, :, lanes(q)] = hi
        esdy_v[1, :, lanes(q)] = low
        for r in range(NZ):
            send1[1, r * NY + q] = loc[RW * r : RW * (r + 1), :]

        def away(dz):
            j = peer(i, dz)
            to_seq(send1.at[1, j], recv1.at[1, me], j, 1)

        for dz in DZ_ORDER:
            if dz:
                away(dz)
        pl.when(i > 0)(lambda: away(0))
        return carry

    lax.fori_loop(0, NY, adj_group, 0)
    own = [
        pltpu.make_async_copy(send1.at[0, me], recv1.at[0, me], own_sem.at[0]),
        pltpu.make_async_copy(send1.at[1, me], recv1.at[1, me], own_sem.at[1]),
        pltpu.make_async_copy(decx.at[0], decr.at[me], own_sem.at[2]),
    ]
    for copy in own:
        copy.start()

    prow_in.wait()
    bi = lax.broadcasted_iota(jnp.int32, (NB, NB), 0)
    bj = lax.broadcasted_iota(jnp.int32, (NB, NB), 1)
    par = jnp.broadcast_to(prow[...], (NB, NB))
    par_col = jnp.sum(jnp.where(bi == bj, par, 0), axis=1, keepdims=True)
    first = jnp.min(jnp.where(par == bi, bj, NB), axis=1, keepdims=True)
    sibling = jnp.min(jnp.where((par == par_col) & (bj > bi), bj, NB), axis=1, keepdims=True)
    tl = lax.broadcasted_iota(jnp.int32, (NB, TILE), 1)
    tab_v[...] = jnp.where(
        tl == 0, first, jnp.where(tl == 1, sibling, jnp.where(par_col < 0, NB, par_col))
    )
    tab = pltpu.make_async_copy(tab_v, tab_s, tab_sem)
    tab.start()

    st_v[...] = lax.dot_general(
        b_ref[...],
        c_ref[...],
        (((1,), (1,)), ((), ())),
        preferred_element_type=f32,
        precision=lax.Precision.HIGHEST,
    )
    mt_v[...] = jnp.zeros_like(mt_v)
    colq_v[...] = jnp.zeros_like(colq_v)
    for h in range(NH):
        crow_v[h] = cum[h : h + 1, :]
        ccol_v[h] = jnp.broadcast_to(cols[:, 4 * NH + h : 4 * NH + h + 1], (ROWS, TILE))
    left = lax.broadcasted_iota(jnp.int32, (ROWS, TILE), 1) < WID
    nil = jnp.zeros((ROWS, TILE), bf16)

    def pair(k, carry):
        span = pl.ds(pl.multiple_of(k * TILE, TILE), TILE)
        xk = x_v[:, span]
        dk = dy_v[:, span]
        xr = pltpu.roll(xk, WID, 1)
        dr = pltpu.roll(dk, WID, 1)
        xs, ds = [], []
        for s in range(2):
            hi, low = halves_of(jnp.where(left, xk, xr) if s == 0 else jnp.where(left, xr, xk))
            both = jnp.where(left, hi, low)
            xs.append(jnp.concatenate([both, both], axis=1))
            ds.append(halves_of(jnp.where(left, dk, dr) if s == 0 else jnp.where(left, dr, dk)))
        dg = [jnp.concatenate(d, axis=1) for d in ds]
        dn = [jnp.where(left, ds[0][0], nil), jnp.where(left, nil, ds[1][0])]
        dx = [jnp.zeros((TILE, TILE), f32) for _ in range(NT)]
        rowq = [[None] * NT, [None] * NT]
        colq = [[None] * NT, [None] * NT]
        for ib in range(NT):
            ts = slice(TILE * ib, TILE * (ib + 1))
            dt = jnp.concatenate([dn[0][ts, :], dn[1][ts, :]], axis=0)
            for jb in range(ib + 1):
                us = slice(TILE * jb, TILE * (jb + 1))
                score = st_v[us, ts]
                total = mt_v[us, ts]
                wide = []
                for s in range(2):
                    h = 2 * k + s
                    g = dot_t(xs[s][us, :], dg[s][ts, :])
                    diff = crow_v[h, :, ts] - ccol_v[h, us, :]
                    if ib == jb:
                        diff = jnp.where(tj >= ti, diff, -1e30)
                    e = jnp.exp2(diff)
                    dsc = e * score
                    total = total + e * g
                    wide.append(dsc.astype(bf16))
                    joint = dsc * g
                    down = jnp.sum(joint, axis=0, keepdims=True)
                    rowq[s][ib] = down if jb == 0 else rowq[s][ib] + down
                    colq[s][jb] = joint if ib == jb else colq[s][jb] + joint
                mt_v[us, ts] = total
                dx[jb] = dx[jb] + dot(jnp.concatenate(wide, axis=1), dt)
        for s in range(2):
            rowq_v[2 * k + s] = jnp.concatenate(rowq[s], axis=1)
        for jb in range(NT):
            us = slice(TILE * jb, TILE * (jb + 1))
            both = colq_v[us, :]
            for s in range(2):
                tot = jnp.sum(colq[s][jb], axis=1, keepdims=True)
                both = jnp.where(tj == 2 * NH + 2 * k + s, tot, both)
            colq_v[us, :] = both
            dx_v[us, span] = dx[jb]
        return carry

    f_v[NB] = jnp.zeros((RW, QW), f32)
    r_v[NB] = jnp.zeros((RW, QW), f32)

    def forward(b, carry):
        state = f_v[tab_s[b, 2]]
        send2[0, b] = state.astype(bf16)
        f_v[b] = recv1[0, b].astype(f32) + decw[b] * state
        return carry

    def backward(k, carry):
        a = NB - 1 - k
        adj = r_v[tab_s[a, 0]]
        send2[1, a] = adj.astype(bf16)
        r_v[a] = recv1[1, a].astype(f32) + decw[a] * adj + r_v[tab_s[a, 1]]
        return carry

    def own2(w):
        return pltpu.make_async_copy(send2.at[w, me], recv2.at[w, me], own_sem.at[3 + w])

    def hand_back(w, k):
        for i in range(NY - 1, -1, -1):
            for dz in DZ_ORDER:
                if i or dz:
                    j = peer(i, dz)
                    to_seq(send2.at[w, j], recv2.at[w, me], j, k + i)
        own2(w).start()

    def stage(g, carry):
        lax.fori_loop(CUT * g, jnp.minimum(CUT * (g + 1), NH // 2), pair, 0)

        @pl.when(g == 0)
        def _():
            tab.wait()
            for copy in own:
                copy.wait()
            settle(recv1.at[0, pl.ds(0, NB - 1)], recv_sem.at[0])
            settle(decr.at[pl.ds(0, NB - 1)], recv_sem.at[2])
            mine = eh + (my_y * (NH // NY) + 2 * NH)
            widen = jnp.where((er == mine) | (er == mine + NH), 1.0, 0.0).astype(bf16)
            dec_rows = jnp.concatenate([decr[b] for b in range(NB)], axis=0).astype(bf16)
            dec_wide = dot(dec_rows, widen)
            for b in range(NB):
                decw[b] = dec_wide[b : b + 1, :]
            lax.fori_loop(0, NB, forward, 0)
            hand_back(0, 9)

        @pl.when(g == 1)
        def _():
            settle(recv1.at[1, pl.ds(0, NB - 1)], recv_sem.at[1])
            lax.fori_loop(0, NB, backward, 0)
            hand_back(1, 9 + NY)

        return carry

    lax.fori_loop(0, 3, stage, 0)

    b_hi, b_lo = halves_of(b_ref[...])
    c_hi, c_lo = halves_of(c_ref[...])
    mt_hi, mt_lo = halves_of(mt_v[...])
    sum_v[0] = dot_0(mt_hi, b_hi) + dot_0(mt_lo, b_hi) + dot_0(mt_hi, b_lo)
    sum_v[1] = dot(mt_hi, c_hi) + dot(mt_lo, c_hi) + dot(mt_hi, c_lo)
    b_two = jnp.concatenate([b_hi, b_lo], axis=1)
    c_two = jnp.concatenate([c_hi, c_lo], axis=1)

    def returned(w, i):
        return jnp.concatenate([recv2[w, r * NY + source(i)] for r in range(NZ)], axis=0)

    def gather(w, pair_v):
        def column_group(k, carry):
            i = NY - 1 - k

            @pl.when(i > 0)
            def _():
                settle(recv2.at[w, pl.ds(0, NZ)], recv_sem.at[9 + NY * w + i])

            @pl.when(i == 0)
            def _():
                own2(w).wait()
                settle(recv2.at[w, pl.ds(0, NZ - 1)], recv_sem.at[9 + NY * w])

            sum_v[w] += both_halves(pair_v, i, returned(w, i))
            return carry

        lax.fori_loop(0, NY, column_group, 0)

    def both_halves(pair_v, i, state):
        span = lanes(source(i))
        return dot_t(pair_v[0, :, span], state) + dot_t(pair_v[1, :, span], state)

    def source(i):
        return lax.rem(my_y + (NY - i), NY)

    def scatter(w, k):
        part_v[w] = sum_v[w].astype(bf16)
        for d in (4, 3, 5, 2, 6, 1, 7):
            to = lax.rem(mp + d, NMP)
            to_mp(part_v.at[w, share_of(to)], rbuf.at[w, mp], to, k)
        copy = pltpu.make_async_copy(part_v.at[w, share_of(mp)], rbuf.at[w, mp], own_sem.at[5 + w])
        copy.start()
        return copy

    def share_of(k):
        return pl.ds(pl.multiple_of(k * SHARE, SHARE), SHARE)

    def spread_share(w, out, own_part, k):
        own_part.wait()
        settle(rbuf.at[w, pl.ds(0, NMP - 1)], recv_sem.at[k])
        share = rbuf[w, 0].astype(f32)
        for d in range(1, NMP):
            share = share + rbuf[w, d].astype(f32)
        out[share_of(mp), :] = share.astype(bf16)
        for d in (4, 3, 5, 2, 6, 1, 7):
            to_mp(out.at[share_of(mp), :], out.at[share_of(mp), :], lax.rem(mp + d, NMP), k + 1)

    gather(0, esdy_v)
    own_dc = scatter(0, 5)
    sel_r = lax.broadcasted_iota(jnp.int32, (QW, TILE), 0) // WID
    sel_l = lax.broadcasted_iota(jnp.int32, (QW, TILE), 1)

    def picks(q, base):
        return jnp.where(sel_l == sel_r + (q * (NH // NY) + base), 1.0, 0.0).astype(bf16)

    def head_terms(i, carry):
        state = returned(0, i)
        chi = dot(c_two, jnp.concatenate([state, state], axis=0))
        head = chi * esdy_v[0, :, lanes(source(i))].astype(f32)
        colq_v[...] += dot(head.astype(bf16), picks(source(i), 0))
        return carry

    lax.fori_loop(0, NY, head_terms, 0)
    spread_share(0, dc_out, own_dc, 5)

    gather(1, eex_v)
    own_db = scatter(1, 7)

    def tail_terms(i, gs):
        q = source(i)
        span = lanes(q)
        adj = returned(1, i)
        bgo = dot(b_two, jnp.concatenate([adj, adj], axis=0))
        dx_v[:, span] = dx_v[:, span] + eexp_v[:, span] * bgo
        eex = eex_v[0, :, span].astype(f32)
        colq_v[...] += dot((bgo * eex).astype(bf16), picks(q, NH))
        both = jnp.sum(adj.astype(f32) * returned(0, i).astype(f32), axis=0, keepdims=True)
        both_hi, both_lo = halves_of(jnp.broadcast_to(both, (8, QW)))
        return gs + dot(both_hi, picks(q, 0)) + dot(both_lo, picks(q, 0))

    gs = lax.fori_loop(0, NY, tail_terms, jnp.zeros((8, NST), f32))
    spread_share(1, db_out, own_db, 7)

    flat = colq_v[...].T
    gs_col = gs.T[0:NH, 0:1]
    head = flat[0:NH]
    tail = flat[NH : 2 * NH]
    colq = flat[2 * NH : 3 * NH]
    since = jnp.where(ti >= tj, 1.0, 0.0).astype(bf16)
    before = jnp.where(ti < tj, 1.0, 0.0).astype(bf16)
    dec = jnp.exp2(last_v[:, 0:1])
    rowq = jnp.concatenate([rowq_v[h] for h in range(NH)], axis=0)
    total = running(rowq - colq + head, since, True) + running(tail, before, False) + dec * gs_col
    dl_ref[...] = jnp.where(live, total, 0.0)

    settle(send1.at[0, pl.ds(0, NB - 1)], send_sem.at[0])
    settle(send1.at[1, pl.ds(0, NB - 1)], send_sem.at[1])
    settle(decr.at[pl.ds(0, NB - 1)], send_sem.at[2])
    for k in range(2 * NY):
        settle(send2.at[0, pl.ds(0, NZ if k % NY else NZ - 1)], send_sem.at[9 + k])
    for w in range(2):
        settle(rbuf.at[w, pl.ds(0, NMP - 1)], send_sem.at[5 + 2 * w])
        settle(rbuf.at[w, pl.ds(0, NMP - 1)], send_sem.at[6 + 2 * w])
    settle(rbuf.at[0, pl.ds(0, NMP - 1)], recv_sem.at[6])
    settle(rbuf.at[1, pl.ds(0, NMP - 1)], recv_sem.at[8])


def finish(xg_ref, db_ref, dc_ref, dl_ref, xg_out, db_out, dc_out, dl_out, db_v, dc_v, sem):
    copies = [pltpu.make_async_copy(xg_ref, xg_out, sem.at[0]), pltpu.make_async_copy(dl_ref, dl_out, sem.at[1])]
    for copy in copies:
        copy.start()
    for k, (low, wide, out) in enumerate(((db_ref, db_v, db_out), (dc_ref, dc_v, dc_out))):
        wide[...] = low[...].astype(f32)
        copy = pltpu.make_async_copy(wide, out, sem.at[2 + k])
        copy.start()
        copies.append(copy)
    for copy in copies:
        copy.wait()


def on_device(x_in, dy_out, b_in, c_in, log_decay, parents, lengths):
    vmem = pl.BlockSpec(memory_space=pltpu.VMEM)
    anywhere = pl.BlockSpec(memory_space=pl.ANY)
    wide = (ROWS, CH)
    dma = pltpu.SemaphoreType.DMA
    given = pl.pallas_call(
        kernel,
        out_shape=(
            pltpu.VMEM(wide, f32),
            pltpu.VMEM((ROWS, NST), bf16),
            pltpu.VMEM((ROWS, NST), bf16),
            pltpu.VMEM((NH, ROWS), f32),
        ),
        in_specs=[anywhere] * 7,
        out_specs=(vmem, vmem, vmem, vmem),
        scratch_shapes=[
            pltpu.SMEM((1, NB), jnp.int32),
            pltpu.VMEM((1, NB), jnp.int32),
            pltpu.VMEM((ROWS, NST), f32),
            pltpu.VMEM((ROWS, NST), f32),
            pltpu.VMEM((NH, ROWS), f32),
            pltpu.VMEM(wide, f32),
            pltpu.VMEM(wide, f32),
            pltpu.VMEM((2, *wide), bf16),
            pltpu.VMEM((2, *wide), bf16),
            pltpu.VMEM(wide, f32),
            pltpu.VMEM((2, NST, ROWS), bf16),
            pltpu.VMEM((2, NST, ROWS), bf16),
            pltpu.VMEM((NH, ROWS, TILE), f32),
            pltpu.VMEM((NH, 1, ROWS), f32),
            pltpu.VMEM((NH, TILE), f32),
            pltpu.VMEM((ROWS, ROWS), f32),
            pltpu.VMEM((ROWS, ROWS), f32),
            pltpu.VMEM((NH, 1, ROWS), f32),
            pltpu.VMEM((ROWS, TILE), f32),
            pltpu.VMEM((NB, TILE), jnp.int32),
            pltpu.SMEM((NB, TILE), jnp.int32),
            pltpu.VMEM((2, NB, RW, QW), bf16),
            pltpu.VMEM((2, NB, RW, QW), bf16),
            pltpu.VMEM((1, 1, NST), f32),
            pltpu.VMEM((NB, 1, NST), f32),
            pltpu.VMEM((NB, 1, QW), f32),
            pltpu.VMEM((NB + 1, RW, QW), f32),
            pltpu.VMEM((NB + 1, RW, QW), f32),
            pltpu.VMEM((2, NB, RW, QW), bf16),
            pltpu.VMEM((2, NB, RW, QW), bf16),
            pltpu.VMEM((2, ROWS, NST), f32),
            pltpu.VMEM((2, ROWS, NST), bf16),
            pltpu.VMEM((2, NMP, SHARE, NST), bf16),
            dma((2 * NY + 5,)),
            dma,
            dma((9 + 2 * NY,)),
            dma((9 + 2 * NY,)),
            dma((7,)),
        ],
        compiler_params=pltpu.CompilerParams(
            collective_id=0, has_side_effects=True, vmem_limit_bytes=52 * 1024 * 1024
        ),
    )(lengths.reshape(1, NB), parents.reshape(1, NB), x_in, dy_out, b_in, c_in, log_decay)
    return tuple(
        pl.pallas_call(
            finish,
            out_shape=(
                jax.ShapeDtypeStruct(wide, f32),
                jax.ShapeDtypeStruct((ROWS, NST), f32),
                jax.ShapeDtypeStruct((ROWS, NST), f32),
                jax.ShapeDtypeStruct((NH, ROWS), f32),
            ),
            in_specs=[vmem] * 4,
            out_specs=(anywhere,) * 4,
            scratch_shapes=[
                pltpu.VMEM((ROWS, NST), f32),
                pltpu.VMEM((ROWS, NST), f32),
                dma((4,)),
            ],
        )(*(pltpu.with_memory_space_constraint(g, pltpu.VMEM) for g in given))
    )


def solution(mesh):
    return jax.shard_map(
        on_device,
        mesh=mesh,
        in_specs=(
            P("seq", "mp"),
            P("seq", "mp"),
            P("seq", None),
            P("seq", None),
            P("mp", "seq"),
            P(),
            P(),
        ),
        out_specs=(P("seq", "mp"), P("seq", None), P("seq", None), P("mp", "seq")),
        check_vma=False,
    )
```

```python
import functools
import math

import jax
import jax.numpy as jnp
from jax import lax
from jax.experimental import pallas as pl
from jax.experimental.pallas import tpu as pltpu
from jax.sharding import PartitionSpec as P

f32 = jnp.float32
bf16 = jnp.bfloat16
MESH = pl.DeviceIdType.MESH
LOG2E = math.log2(math.e)

ROWS = 512
NST = 128
NH = 16
WID = 64
CH = NH * WID
TILE = 128
NT = ROWS // TILE
NY = 4
NZ = 8
NB = NY * NZ
QW = CH // NY
RW = NST // NZ
NMP = 8
SHARE = ROWS // NMP
CUT = 3
DZ_ORDER = (4, 3, 5, 2, 6, 1, 7, 0)


def dot(a, b):
    return jnp.dot(a, b, preferred_element_type=f32)


def dot_t(a, b):
    return lax.dot_general(a, b, (((1,), (1,)), ((), ())), preferred_element_type=f32)


def dot_0(a, b):
    return lax.dot_general(a, b, (((0,), (0,)), ((), ())), preferred_element_type=f32)


def split3(v):
    hi = v.astype(bf16)
    rest = v - hi.astype(f32)
    mid = rest.astype(bf16)
    low = (rest - mid.astype(f32)).astype(bf16)
    return hi, mid, low


def running(v, tri, reverse):
    tall = jnp.concatenate([v[:, TILE * i : TILE * (i + 1)] for i in range(NT)], axis=0)
    hi, mid, low = split3(tall)
    part = dot(hi, tri) + dot(mid, tri) + dot(low, tri)
    whole = jnp.sum(tall, axis=1, keepdims=True)
    pieces = [None] * NT
    carry = jnp.zeros((NH, 1), f32)
    order = range(NT - 1, -1, -1) if reverse else range(NT)
    for i in order:
        rows = slice(NH * i, NH * (i + 1))
        pieces[i] = part[rows] + carry
        carry = carry + whole[rows]
    return jnp.concatenate(pieces, axis=1)


def halves_of(v):
    hi = v.astype(bf16)
    return hi, (v - hi.astype(f32)).astype(bf16)


def kernel(
    lengths_hbm,
    prow_hbm,
    x_hbm,
    dy_hbm,
    b_hbm,
    c_hbm,
    logd_hbm,
    dx_v,
    db_out,
    dc_out,
    dl_ref,
    lengths,
    prow,
    b_ref,
    c_ref,
    logd_ref,
    x_v,
    dy_v,
    eex_v,
    esdy_v,
    eexp_v,
    bt_v,
    ct_v,
    ccol_v,
    crow_v,
    last_v,
    st_v,
    mt_v,
    rowq_v,
    colq_v,
    tab_v,
    tab_s,
    send1,
    recv1,
    decx,
    decr,
    decw,
    f_v,
    r_v,
    send2,
    recv2,
    sum_v,
    part_v,
    rbuf,
    load_sem,
    tab_sem,
    send_sem,
    recv_sem,
    own_sem,
):
    me = lax.axis_index("seq")
    mp = lax.axis_index("mp")
    my_y = lax.rem(me, NY)
    my_z = me // NY

    def group(i):
        return lax.rem(my_y + i, NY)

    def peer(i, dz):
        return lax.rem(my_z + dz, NZ) * NY + group(i)

    def lanes(q):
        return pl.ds(pl.multiple_of(q * QW, QW), QW)

    def to_seq(src, dst, j, k):
        pltpu.make_async_remote_copy(
            src_ref=src,
            dst_ref=dst,
            send_sem=send_sem.at[k],
            recv_sem=recv_sem.at[k],
            device_id={"seq": j},
            device_id_type=MESH,
        ).start()

    def to_mp(src, dst, j, k):
        pltpu.make_async_remote_copy(
            src_ref=src,
            dst_ref=dst,
            send_sem=send_sem.at[k],
            recv_sem=recv_sem.at[k],
            device_id={"mp": j},
            device_id_type=MESH,
        ).start()

    def settle(like, sem):
        pltpu.make_async_copy(like, like, sem).wait()

    barrier = pltpu.get_barrier_semaphore()
    for i in range(NY):
        for dz in DZ_ORDER:
            if i or dz:
                pl.semaphore_signal(barrier, inc=1, device_id={"seq": peer(i, dz)}, device_id_type=MESH)
    for k in range(1, NMP):
        pl.semaphore_signal(barrier, inc=1, device_id={"mp": lax.rem(mp + k, NMP)}, device_id_type=MESH)

    loads = []

    def load(src, dst):
        copy = pltpu.make_async_copy(src, dst, load_sem.at[len(loads)])
        copy.start()
        loads.append(copy)
        return copy

    logd_in = load(logd_hbm, logd_ref)
    lengths_in = load(lengths_hbm, lengths)
    b_in = load(b_hbm, b_ref)
    x_in = [load(x_hbm.at[:, lanes(group(i))], x_v.at[:, lanes(group(i))]) for i in range(NY)]

    c_in = load(c_hbm, c_ref)
    dy_in = [load(dy_hbm.at[:, lanes(group(i))], dy_v.at[:, lanes(group(i))]) for i in range(NY)]
    prow_in = load(prow_hbm, prow)

    lengths_in.wait()
    length = lengths[0, me]
    logd_in.wait()

    ti = lax.broadcasted_iota(jnp.int32, (TILE, TILE), 0)
    tj = lax.broadcasted_iota(jnp.int32, (TILE, TILE), 1)
    upto = jnp.where(ti <= tj, 1.0, 0.0).astype(bf16)
    lane = lax.broadcasted_iota(jnp.int32, (NH, ROWS), 1)
    live = lane < length
    logd = jnp.where(live, logd_ref[...] * LOG2E, 0.0)
    cum = running(logd, upto, False)
    last = cum[:, ROWS - 1 : ROWS]
    last_v[...] = jnp.broadcast_to(last, (NH, TILE))
    ee = jnp.where(live, jnp.exp2(last - cum), 0.0)
    es = jnp.exp2(cum)
    ee_hi = ee.astype(bf16).astype(f32)
    es_hi = es.astype(bf16).astype(f32)
    stack = jnp.concatenate(
        [ee_hi, ee - ee_hi, es_hi, es - es_hi, cum, jnp.zeros((NST - 5 * NH, ROWS), f32)], axis=0
    )
    cols = stack.T
    decx[0] = cols[ROWS - 1 :, :]
    cols_b = cols.astype(bf16)
    b_in.wait()
    bt_hi, bt_lo = halves_of(b_ref[...].T)
    bt_v[0] = bt_hi
    bt_v[1] = bt_lo

    er = lax.broadcasted_iota(jnp.int32, (NST, QW), 0)
    eh = lax.broadcasted_iota(jnp.int32, (NST, QW), 1) // WID

    def spread(q, base):
        head = eh + (q * (NH // NY) + base)
        return dot(cols_b, jnp.where((er == head) | (er == head + NH), 1.0, 0.0).astype(bf16))

    def state_of(t_v, wide):
        hi, low = halves_of(wide)
        total = dot(t_v[0], hi) + dot(t_v[1], hi) + dot(t_v[0], low)
        return hi, low, total.astype(bf16)

    def end_group(i, carry):
        q = group(i)
        e_wide = spread(q, 0)
        eexp_v[:, lanes(q)] = e_wide
        pltpu.make_async_copy(x_hbm.at[:, lanes(q)], x_v.at[:, lanes(q)], load_sem.at[3 + i]).wait()
        hi, low, loc = state_of(bt_v, x_v[:, lanes(q)] * e_wide)
        eex_v[0, :, lanes(q)] = hi
        eex_v[1, :, lanes(q)] = low
        for r in range(NZ):
            send1[0, r * NY + q] = loc[RW * r : RW * (r + 1), :]

        @pl.when(i == 0)
        def _():
            pl.semaphore_wait(barrier, NB - 1 + NMP - 1)

        def away(dz):
            j = peer(i, dz)
            to_seq(decx.at[0], decr.at[me], j, 2)
            to_seq(send1.at[0, j], recv1.at[0, me], j, 0)

        for dz in DZ_ORDER:
            if dz:
                away(dz)
        pl.when(i > 0)(lambda: away(0))
        return carry

    lax.fori_loop(0, NY, end_group, 0)

    c_in.wait()
    ct_hi, ct_lo = halves_of(c_ref[...].T)
    ct_v[0] = ct_hi
    ct_v[1] = ct_lo
    row_live = lax.broadcasted_iota(jnp.int32, (ROWS, QW), 0) < length
    def adj_group(i, carry):
        q = group(i)
        s_wide = spread(q, 2 * NH)
        pltpu.make_async_copy(dy_hbm.at[:, lanes(q)], dy_v.at[:, lanes(q)], load_sem.at[4 + NY + i]).wait()
        dy = jnp.where(row_live, dy_v[:, lanes(q)], 0.0)
        dy_v[:, lanes(q)] = dy
        hi, low, loc = state_of(ct_v, dy * s_wide)
        esdy_v[0, :, lanes(q)] = hi
        esdy_v[1, :, lanes(q)] = low
        for r in range(NZ):
            send1[1, r * NY + q] = loc[RW * r : RW * (r + 1), :]

        def away(dz):
            j = peer(i, dz)
            to_seq(send1.at[1, j], recv1.at[1, me], j, 1)

        for dz in DZ_ORDER:
            if dz:
                away(dz)
        pl.when(i > 0)(lambda: away(0))
        return carry

    lax.fori_loop(0, NY, adj_group, 0)
    own = [
        pltpu.make_async_copy(send1.at[0, me], recv1.at[0, me], own_sem.at[0]),
        pltpu.make_async_copy(send1.at[1, me], recv1.at[1, me], own_sem.at[1]),
        pltpu.make_async_copy(decx.at[0], decr.at[me], own_sem.at[2]),
    ]
    for copy in own:
        copy.start()

    prow_in.wait()
    bi = lax.broadcasted_iota(jnp.int32, (NB, NB), 0)
    bj = lax.broadcasted_iota(jnp.int32, (NB, NB), 1)
    par = jnp.broadcast_to(prow[...], (NB, NB))
    par_col = jnp.sum(jnp.where(bi == bj, par, 0), axis=1, keepdims=True)
    first = jnp.min(jnp.where(par == bi, bj, NB), axis=1, keepdims=True)
    sibling = jnp.min(jnp.where((par == par_col) & (bj > bi), bj, NB), axis=1, keepdims=True)
    tl = lax.broadcasted_iota(jnp.int32, (NB, TILE), 1)
    tab_v[...] = jnp.where(
        tl == 0, first, jnp.where(tl == 1, sibling, jnp.where(par_col < 0, NB, par_col))
    )
    tab = pltpu.make_async_copy(tab_v, tab_s, tab_sem)
    tab.start()

    st_v[...] = lax.dot_general(
        b_ref[...],
        c_ref[...],
        (((1,), (1,)), ((), ())),
        preferred_element_type=f32,
        precision=lax.Precision.HIGHEST,
    )
    mt_v[...] = jnp.zeros_like(mt_v)
    colq_v[...] = jnp.zeros_like(colq_v)
    for h in range(NH):
        crow_v[h] = cum[h : h + 1, :]
        ccol_v[h] = jnp.broadcast_to(cols[:, 4 * NH + h : 4 * NH + h + 1], (ROWS, TILE))
    left = lax.broadcasted_iota(jnp.int32, (ROWS, TILE), 1) < WID
    nil = jnp.zeros((ROWS, TILE), bf16)

    def pair(k, carry):
        span = pl.ds(pl.multiple_of(k * TILE, TILE), TILE)
        xk = x_v[:, span]
        dk = dy_v[:, span]
        xr = pltpu.roll(xk, WID, 1)
        dr = pltpu.roll(dk, WID, 1)
        xs, ds = [], []
        for s in range(2):
            hi, low = halves_of(jnp.where(left, xk, xr) if s == 0 else jnp.where(left, xr, xk))
            both = jnp.where(left, hi, low)
            xs.append(jnp.concatenate([both, both], axis=1))
            ds.append(halves_of(jnp.where(left, dk, dr) if s == 0 else jnp.where(left, dr, dk)))
        dg = [jnp.concatenate(d, axis=1) for d in ds]
        dn = [jnp.where(left, ds[0][0], nil), jnp.where(left, nil, ds[1][0])]
        dx = [jnp.zeros((TILE, TILE), f32) for _ in range(NT)]
        rowq = [[None] * NT, [None] * NT]
        colq = [[None] * NT, [None] * NT]
        for ib in range(NT):
            ts = slice(TILE * ib, TILE * (ib + 1))
            dt = jnp.concatenate([dn[0][ts, :], dn[1][ts, :]], axis=0)
            for jb in range(ib + 1):
                us = slice(TILE * jb, TILE * (jb + 1))
                score = st_v[us, ts]
                total = mt_v[us, ts]
                wide = []
                for s in range(2):
                    h = 2 * k + s
                    g = dot_t(xs[s][us, :], dg[s][ts, :])
                    diff = crow_v[h, :, ts] - ccol_v[h, us, :]
                    if ib == jb:
                        diff = jnp.where(tj >= ti, diff, -1e30)
                    e = jnp.exp2(diff)
                    dsc = e * score
                    total = total + e * g
                    wide.append(dsc.astype(bf16))
                    joint = dsc * g
                    down = jnp.sum(joint, axis=0, keepdims=True)
                    rowq[s][ib] = down if jb == 0 else rowq[s][ib] + down
                    colq[s][jb] = joint if ib == jb else colq[s][jb] + joint
                mt_v[us, ts] = total
                dx[jb] = dx[jb] + dot(jnp.concatenate(wide, axis=1), dt)
        for s in range(2):
            rowq_v[2 * k + s] = jnp.concatenate(rowq[s], axis=1)
        for jb in range(NT):
            us = slice(TILE * jb, TILE * (jb + 1))
            both = colq_v[us, :]
            for s in range(2):
                tot = jnp.sum(colq[s][jb], axis=1, keepdims=True)
                both = jnp.where(tj == 2 * NH + 2 * k + s, tot, both)
            colq_v[us, :] = both
            dx_v[us, span] = dx[jb]
        return carry

    f_v[NB] = jnp.zeros((RW, QW), f32)
    r_v[NB] = jnp.zeros((RW, QW), f32)

    def forward(b, carry):
        state = f_v[tab_s[b, 2]]
        send2[0, b] = state.astype(bf16)
        f_v[b] = recv1[0, b].astype(f32) + decw[b] * state
        return carry

    def backward(k, carry):
        a = NB - 1 - k
        adj = r_v[tab_s[a, 0]]
        send2[1, a] = adj.astype(bf16)
        r_v[a] = recv1[1, a].astype(f32) + decw[a] * adj + r_v[tab_s[a, 1]]
        return carry

    def own2(w):
        return pltpu.make_async_copy(send2.at[w, me], recv2.at[w, me], own_sem.at[3 + w])

    def hand_back(w, k):
        for i in range(NY - 1, -1, -1):
            for dz in DZ_ORDER:
                if i or dz:
                    j = peer(i, dz)
                    to_seq(send2.at[w, j], recv2.at[w, me], j, k + i)
        own2(w).start()

    def stage(g, carry):
        lax.fori_loop(CUT * g, jnp.minimum(CUT * (g + 1), NH // 2), pair, 0)

        @pl.when(g == 0)
        def _():
            tab.wait()
            for copy in own:
                copy.wait()
            settle(recv1.at[0, pl.ds(0, NB - 1)], recv_sem.at[0])
            settle(decr.at[pl.ds(0, NB - 1)], recv_sem.at[2])
            mine = eh + (my_y * (NH // NY) + 2 * NH)
            widen = jnp.where((er == mine) | (er == mine + NH), 1.0, 0.0).astype(bf16)
            dec_rows = jnp.concatenate([decr[b] for b in range(NB)], axis=0).astype(bf16)
            dec_wide = dot(dec_rows, widen)
            for b in range(NB):
                decw[b] = dec_wide[b : b + 1, :]
            lax.fori_loop(0, NB, forward, 0)
            hand_back(0, 9)

        @pl.when(g == 1)
        def _():
            settle(recv1.at[1, pl.ds(0, NB - 1)], recv_sem.at[1])
            lax.fori_loop(0, NB, backward, 0)
            hand_back(1, 9 + NY)

        return carry

    lax.fori_loop(0, 3, stage, 0)

    b_hi, b_lo = halves_of(b_ref[...])
    c_hi, c_lo = halves_of(c_ref[...])
    mt_hi, mt_lo = halves_of(mt_v[...])
    sum_v[0] = dot_0(mt_hi, b_hi) + dot_0(mt_lo, b_hi) + dot_0(mt_hi, b_lo)
    sum_v[1] = dot(mt_hi, c_hi) + dot(mt_lo, c_hi) + dot(mt_hi, c_lo)
    b_two = jnp.concatenate([b_hi, b_lo], axis=1)
    c_two = jnp.concatenate([c_hi, c_lo], axis=1)

    def returned(w, i):
        return jnp.concatenate([recv2[w, r * NY + source(i)] for r in range(NZ)], axis=0)

    def gather(w, pair_v):
        def column_group(k, carry):
            i = NY - 1 - k

            @pl.when(i > 0)
            def _():
                settle(recv2.at[w, pl.ds(0, NZ)], recv_sem.at[9 + NY * w + i])

            @pl.when(i == 0)
            def _():
                own2(w).wait()
                settle(recv2.at[w, pl.ds(0, NZ - 1)], recv_sem.at[9 + NY * w])

            sum_v[w] += both_halves(pair_v, i, returned(w, i))
            return carry

        lax.fori_loop(0, NY, column_group, 0)

    def both_halves(pair_v, i, state):
        span = lanes(source(i))
        both = jnp.concatenate([pair_v[0, :, span], pair_v[1, :, span]], axis=1)
        return dot_t(both, jnp.concatenate([state, state], axis=1))

    def source(i):
        return lax.rem(my_y + (NY - i), NY)

    def scatter(w, k):
        part_v[w] = sum_v[w].astype(bf16)
        for d in (4, 3, 5, 2, 6, 1, 7):
            to = lax.rem(mp + d, NMP)
            to_mp(part_v.at[w, share_of(to)], rbuf.at[w, mp], to, k)
        copy = pltpu.make_async_copy(part_v.at[w, share_of(mp)], rbuf.at[w, mp], own_sem.at[5 + w])
        copy.start()
        return copy

    def share_of(k):
        return pl.ds(pl.multiple_of(k * SHARE, SHARE), SHARE)

    def spread_share(w, out, own_part, k):
        own_part.wait()
        settle(rbuf.at[w, pl.ds(0, NMP - 1)], recv_sem.at[k])
        share = rbuf[w, 0].astype(f32)
        for d in range(1, NMP):
            share = share + rbuf[w, d].astype(f32)
        out[share_of(mp), :] = share.astype(bf16)
        for d in (4, 3, 5, 2, 6, 1, 7):
            to_mp(out.at[share_of(mp), :], out.at[share_of(mp), :], lax.rem(mp + d, NMP), k + 1)

    gather(0, esdy_v)
    own_dc = scatter(0, 5)
    sel_r = lax.broadcasted_iota(jnp.int32, (QW, TILE), 0) // WID
    sel_l = lax.broadcasted_iota(jnp.int32, (QW, TILE), 1)

    def picks(q, base):
        return jnp.where(sel_l == sel_r + (q * (NH // NY) + base), 1.0, 0.0).astype(bf16)

    def head_terms(i, carry):
        state = returned(0, i)
        chi = dot(c_two, jnp.concatenate([state, state], axis=0))
        head = chi * esdy_v[0, :, lanes(source(i))].astype(f32)
        colq_v[...] += dot(head.astype(bf16), picks(source(i), 0))
        return carry

    lax.fori_loop(0, NY, head_terms, 0)
    spread_share(0, dc_out, own_dc, 5)

    gather(1, eex_v)
    own_db = scatter(1, 7)

    def tail_terms(i, gs):
        q = source(i)
        span = lanes(q)
        adj = returned(1, i)
        bgo = dot(b_two, jnp.concatenate([adj, adj], axis=0))
        dx_v[:, span] = dx_v[:, span] + eexp_v[:, span] * bgo
        eex = eex_v[0, :, span].astype(f32)
        colq_v[...] += dot((bgo * eex).astype(bf16), picks(q, NH))
        both = jnp.sum(adj.astype(f32) * returned(0, i).astype(f32), axis=0, keepdims=True)
        both_hi, both_lo = halves_of(jnp.broadcast_to(both, (8, QW)))
        return gs + dot(both_hi, picks(q, 0)) + dot(both_lo, picks(q, 0))

    gs = lax.fori_loop(0, NY, tail_terms, jnp.zeros((8, NST), f32))
    spread_share(1, db_out, own_db, 7)

    flat = colq_v[...].T
    gs_col = gs.T[0:NH, 0:1]
    head = flat[0:NH]
    tail = flat[NH : 2 * NH]
    colq = flat[2 * NH : 3 * NH]
    since = jnp.where(ti >= tj, 1.0, 0.0).astype(bf16)
    before = jnp.where(ti < tj, 1.0, 0.0).astype(bf16)
    dec = jnp.exp2(last_v[:, 0:1])
    rowq = jnp.concatenate([rowq_v[h] for h in range(NH)], axis=0)
    total = running(rowq - colq + head, since, True) + running(tail, before, False) + dec * gs_col
    dl_ref[...] = jnp.where(live, total, 0.0)

    settle(send1.at[0, pl.ds(0, NB - 1)], send_sem.at[0])
    settle(send1.at[1, pl.ds(0, NB - 1)], send_sem.at[1])
    settle(decr.at[pl.ds(0, NB - 1)], send_sem.at[2])
    for k in range(2 * NY):
        settle(send2.at[0, pl.ds(0, NZ if k % NY else NZ - 1)], send_sem.at[9 + k])
    for w in range(2):
        settle(rbuf.at[w, pl.ds(0, NMP - 1)], send_sem.at[5 + 2 * w])
        settle(rbuf.at[w, pl.ds(0, NMP - 1)], send_sem.at[6 + 2 * w])
    settle(rbuf.at[0, pl.ds(0, NMP - 1)], recv_sem.at[6])
    settle(rbuf.at[1, pl.ds(0, NMP - 1)], recv_sem.at[8])


def finish(xg_ref, db_ref, dc_ref, dl_ref, xg_out, db_out, dc_out, dl_out, db_v, dc_v, sem):
    copies = [pltpu.make_async_copy(xg_ref, xg_out, sem.at[0]), pltpu.make_async_copy(dl_ref, dl_out, sem.at[1])]
    for copy in copies:
        copy.start()
    for k, (low, wide, out) in enumerate(((db_ref, db_v, db_out), (dc_ref, dc_v, dc_out))):
        wide[...] = low[...].astype(f32)
        copy = pltpu.make_async_copy(wide, out, sem.at[2 + k])
        copy.start()
        copies.append(copy)
    for copy in copies:
        copy.wait()


def on_device(x_in, dy_out, b_in, c_in, log_decay, parents, lengths):
    vmem = pl.BlockSpec(memory_space=pltpu.VMEM)
    anywhere = pl.BlockSpec(memory_space=pl.ANY)
    wide = (ROWS, CH)
    dma = pltpu.SemaphoreType.DMA
    given = pl.pallas_call(
        kernel,
        out_shape=(
            pltpu.VMEM(wide, f32),
            pltpu.VMEM((ROWS, NST), bf16),
            pltpu.VMEM((ROWS, NST), bf16),
            pltpu.VMEM((NH, ROWS), f32),
        ),
        in_specs=[anywhere] * 7,
        out_specs=(vmem, vmem, vmem, vmem),
        scratch_shapes=[
            pltpu.SMEM((1, NB), jnp.int32),
            pltpu.VMEM((1, NB), jnp.int32),
            pltpu.VMEM((ROWS, NST), f32),
            pltpu.VMEM((ROWS, NST), f32),
            pltpu.VMEM((NH, ROWS), f32),
            pltpu.VMEM(wide, f32),
            pltpu.VMEM(wide, f32),
            pltpu.VMEM((2, *wide), bf16),
            pltpu.VMEM((2, *wide), bf16),
            pltpu.VMEM(wide, f32),
            pltpu.VMEM((2, NST, ROWS), bf16),
            pltpu.VMEM((2, NST, ROWS), bf16),
            pltpu.VMEM((NH, ROWS, TILE), f32),
            pltpu.VMEM((NH, 1, ROWS), f32),
            pltpu.VMEM((NH, TILE), f32),
            pltpu.VMEM((ROWS, ROWS), f32),
            pltpu.VMEM((ROWS, ROWS), f32),
            pltpu.VMEM((NH, 1, ROWS), f32),
            pltpu.VMEM((ROWS, TILE), f32),
            pltpu.VMEM((NB, TILE), jnp.int32),
            pltpu.SMEM((NB, TILE), jnp.int32),
            pltpu.VMEM((2, NB, RW, QW), bf16),
            pltpu.VMEM((2, NB, RW, QW), bf16),
            pltpu.VMEM((1, 1, NST), f32),
            pltpu.VMEM((NB, 1, NST), f32),
            pltpu.VMEM((NB, 1, QW), f32),
            pltpu.VMEM((NB + 1, RW, QW), f32),
            pltpu.VMEM((NB + 1, RW, QW), f32),
            pltpu.VMEM((2, NB, RW, QW), bf16),
            pltpu.VMEM((2, NB, RW, QW), bf16),
            pltpu.VMEM((2, ROWS, NST), f32),
            pltpu.VMEM((2, ROWS, NST), bf16),
            pltpu.VMEM((2, NMP, SHARE, NST), bf16),
            dma((2 * NY + 5,)),
            dma,
            dma((9 + 2 * NY,)),
            dma((9 + 2 * NY,)),
            dma((7,)),
        ],
        compiler_params=pltpu.CompilerParams(
            collective_id=0, has_side_effects=True, vmem_limit_bytes=52 * 1024 * 1024
        ),
    )(lengths.reshape(1, NB), parents.reshape(1, NB), x_in, dy_out, b_in, c_in, log_decay)
    return tuple(
        pl.pallas_call(
            finish,
            out_shape=(
                jax.ShapeDtypeStruct(wide, f32),
                jax.ShapeDtypeStruct((ROWS, NST), f32),
                jax.ShapeDtypeStruct((ROWS, NST), f32),
                jax.ShapeDtypeStruct((NH, ROWS), f32),
            ),
            in_specs=[vmem] * 4,
            out_specs=(anywhere,) * 4,
            scratch_shapes=[
                pltpu.VMEM((ROWS, NST), f32),
                pltpu.VMEM((ROWS, NST), f32),
                dma((4,)),
            ],
        )(*(pltpu.with_memory_space_constraint(g, pltpu.VMEM) for g in given))
    )


def solution(mesh):
    return jax.shard_map(
        on_device,
        mesh=mesh,
        in_specs=(
            P("seq", "mp"),
            P("seq", "mp"),
            P("seq", None),
            P("seq", None),
            P("mp", "seq"),
            P(),
            P(),
        ),
        out_specs=(P("seq", "mp"), P("seq", None), P("seq", None), P("mp", "seq")),
        check_vma=False,
    )
```
